32 devices in a mesh: rep: 2 (over y), own: 4 (over z), tp: 4 (over x, core).
Axes of the slice: x: 2, y: 2, z: 4, core: 2. Of those that a mesh axis runs over, the one named last changes fastest.
Arguments:
- tokens: bfloat16 [4096, 8192], P(('rep', 'own'), 'tp'), parts along dimension 0, may hold values from -6 to 6
- token_adapter_index: int32 [4096], P(('rep', 'own')), parts along dimension 0, may hold values from 0 to 31, as said below
- adapter_storage_row: int32 [64], P('rep'), parts along dimension 0, may hold values from 0 to 31, as said below
- value_matrix: bfloat16 [8192, 512], P('tp'), may hold values from -0.0625 to 0.0625
- down_weight_stored: bfloat16 [64, 8192, 64], P(('rep', 'own'), 'tp'), parts along dimension 0, may hold values from -0.0625 to 0.0625
- up_weight_stored: bfloat16 [64, 64, 512], P(('rep', 'own'), None, 'tp'), parts along dimension 0, may hold values from -0.75 to 0.75
Outputs:
- values: bfloat16 [4096, 512], P(('rep', 'own'), 'tp'), parts along dimension 0
The draws below stay inside these ranges and needn't reach their ends.
There are 2 independent parts, one for each index of `rep`. The reference program is written for one: setup_inputs(seed, part) draws one part's arguments, and reference() takes and returns one part's arrays. A program takes and returns all parts, laid end to end along the dimension named above; an argument that names none is the same for every part. Nothing has to cross between parts.
Inputs may be any that keep to these rules, and one draw needn't show every extreme that they name: Row r of down_weight_stored and up_weight_stored is entry r % 8 of owner r // 8; adapter_storage_row is a permutation. `token_adapter_index`: A token's adapter lies on owner adapter_storage_row[id] // 8. The tokens of one group come in runs of up to 4 tokens that share an adapter. From one group at most 256 tokens use adapters of one owner, and some owner receives exactly 256 tokens from every group.
All inputs are finite; a program needn't handle non-finite values.
Results may differ from the reference program's by a relative error of at most 0.001.
Values may be sent and summed in bfloat16 or wider, within the bound.
No kernel may reach another device: no remote copies, remote signals or barrier semaphores. Data moves between devices by JAX's collectives and lax.ppermute only.
A program may use at most 64 MiB of HBM per device.

```python
import jax
import jax.numpy as jnp
from jax import lax

MODEL_WIDTH = 8192
VALUE_COLUMNS = 512
ADAPTER_RANK = 64
CAP = 4
TOK_DEV = 512
ADAPT_DEV = 8
TOKEN_COUNT = 2048
ADAPTER_COUNT = 32


def storage_layout(key):
    return jax.random.permutation(jax.random.fold_in(key, 11), ADAPTER_COUNT).astype(jnp.int32)


def draw_adapter_storage_row(key, part):
    return storage_layout(key)


def draw_token_adapter_index(key, part):
    row_adapter = jnp.argsort(storage_layout(key)).astype(jnp.int32)
    key = jax.random.fold_in(key, 5)
    owner_key, order_key, length_key, local_key = jax.random.split(key, 4)
    groups = TOKEN_COUNT // TOK_DEV
    request_count = 2 * TOK_DEV // CAP
    full_owner = jax.random.randint(owner_key, (), 0, groups).astype(jnp.int32)
    order_keys = jax.random.split(order_key, groups)
    shuffled = jax.vmap(lambda group_key: jax.random.permutation(group_key, groups - 1))(order_keys)
    offsets = jnp.concatenate([jnp.zeros((groups, 1), jnp.int32), 1 + shuffled.astype(jnp.int32)], axis=1)
    slot_index = jnp.arange(request_count, dtype=jnp.int32) % groups
    request_owner = (full_owner + offsets[:, slot_index]) % groups
    halves = jax.random.randint(length_key, (groups, request_count // 2), 0, CAP + 1).astype(jnp.int32)
    forced = 2 * jnp.arange(request_count // 2, dtype=jnp.int32) % groups == 0
    halves = jnp.where(forced[None, :], CAP, halves)
    lengths = jnp.stack([halves, CAP - halves], axis=2).reshape(groups, request_count)
    local_pick = jax.random.randint(local_key, (groups, request_count), 0, ADAPT_DEV).astype(jnp.int32)
    request_adapter = row_adapter[request_owner * ADAPT_DEV + local_pick]
    ends = jnp.cumsum(lengths, axis=1)
    positions = jnp.arange(TOK_DEV, dtype=jnp.int32)
    request_of = jnp.sum((ends[:, None, :] <= positions[None, :, None]).astype(jnp.int32), axis=2)
    picked = jnp.take_along_axis(request_adapter, request_of, axis=1)
    return picked.reshape(TOKEN_COUNT).astype(jnp.int32)


def levels(rng, extent, cuts, least, top_value):
    def one(dim, parts):
        steps = jax.random.uniform(jax.random.fold_in(jax.random.fold_in(rng, 6), dim), (parts,), jnp.float32, least / len(cuts), top_value / len(cuts))
        return jnp.repeat(jnp.exp(steps), extent[dim] // parts).reshape((-1,) + (1,) * (len(extent) - dim - 1))

    level = one(*cuts[0])
    for cut in cuts[1:]:
        level = level * one(*cut)
    return level


def scatter_about(own_key, shape, spread, reach, shards=(), held_as=jnp.bfloat16):
    result = spread * jax.random.normal(own_key, shape, jnp.float32)
    if shards:
        result = result * levels(own_key, shape, shards, -0.22, 0.18)
    return jnp.clip(result, -reach, reach).astype(held_as)


def setup_inputs(seed: int = 0, part: int = 0) -> dict:
    key_list = jax.random.split(jax.random.key(seed), 7)
    part_keys = jax.random.split(jax.random.fold_in(key_list[6], part), 7)
    tokens = scatter_about(part_keys[0], (TOKEN_COUNT, MODEL_WIDTH), 1.0, 6.0, ((0, 4), (1, 4)))
    token_adapter_index = draw_token_adapter_index(jax.random.fold_in(jax.random.fold_in(key_list[6], part), 71), part)
    adapter_storage_row = draw_adapter_storage_row(jax.random.fold_in(jax.random.fold_in(key_list[6], part), 71), part)
    value_matrix = scatter_about(key_list[3], (MODEL_WIDTH, VALUE_COLUMNS), MODEL_WIDTH ** -0.5, 0.0625, ((0, 4),))
    down_weight_stored = scatter_about(part_keys[4], (ADAPTER_COUNT, MODEL_WIDTH, ADAPTER_RANK), MODEL_WIDTH ** -0.5, 0.0625, ((0, 4), (1, 4)))
    up_weight_stored = scatter_about(part_keys[5], (ADAPTER_COUNT, ADAPTER_RANK, VALUE_COLUMNS), ADAPTER_RANK ** -0.5, 0.75, ((0, 4), (2, 4)))
    return dict(tokens=tokens, token_adapter_index=token_adapter_index, adapter_storage_row=adapter_storage_row, value_matrix=value_matrix, down_weight_stored=down_weight_stored, up_weight_stored=up_weight_stored)


ADAPTER_SCALE = 0.5


def reference(tokens, token_adapter_index, adapter_storage_row, value_matrix, down_weight_stored, up_weight_stored):
    base_product = jnp.dot(tokens, value_matrix, preferred_element_type=jnp.float32)
    storage = adapter_storage_row[token_adapter_index].astype(jnp.int32)
    rows_per_block = 64

    def single_block(block_index):
        block_start = block_index * rows_per_block
        rows_in = lax.dynamic_slice_in_dim(tokens, block_start, rows_per_block, 0).astype(jnp.float32)
        selected_rows = lax.dynamic_slice_in_dim(storage, block_start, rows_per_block, 0)
        down_weight_rows = down_weight_stored[selected_rows].astype(jnp.float32)
        up_weight_rows = up_weight_stored[selected_rows].astype(jnp.float32)
        low_part = jnp.einsum("td,tdr->tr", rows_in, down_weight_rows, precision=lax.Precision.HIGHEST)
        return jnp.einsum("tr,trv->tv", low_part, up_weight_rows, precision=lax.Precision.HIGHEST)

    adapter_product = lax.map(single_block, jnp.arange(TOKEN_COUNT // rows_per_block, dtype=jnp.int32))
    adapter_product = adapter_product.reshape(TOKEN_COUNT, VALUE_COLUMNS)
    return (base_product + ADAPTER_SCALE * adapter_product).astype(jnp.bfloat16)
```

```python
import functools

import jax
import jax.numpy as jnp
from jax import lax
from jax.experimental import pallas as pl
from jax.experimental.pallas import tpu as pltpu
from jax.sharding import PartitionSpec as P

CAP = 4
ADAPTER_SCALE = 0.5
LINE = 4
BF16 = jnp.bfloat16
F32 = jnp.float32
VMEM_LIMIT = 48 * 2**20
CHEAP = pl.CostEstimate(flops=1, bytes_accessed=1, transcendentals=0)


def params(**kw):
    return pltpu.CompilerParams(vmem_limit_bytes=VMEM_LIMIT, **kw)


def iota(shape, dim):
    return lax.broadcasted_iota(jnp.int32, shape, dim)


def dot(a, b, dims=((1,), (0,))):
    return lax.dot_general(a, b, (dims, ((), ())), preferred_element_type=F32)


def split_bf16(x):
    high = x.astype(BF16)
    return high, (x - high.astype(F32)).astype(BF16)


def one_hot(mask):
    return mask.astype(F32).astype(BF16)


IN_VMEM = pl.BlockSpec(memory_space=pltpu.VMEM)
IN_SMEM = pl.BlockSpec(memory_space=pltpu.SMEM)


def storage_of(index_row, storage_row):
    adapters = storage_row.shape[1]
    square = (adapters, adapters)
    diagonal = jnp.where(iota(square, 0) == iota(square, 1), storage_row.astype(F32), 0.0)
    column = jnp.sum(diagonal, axis=1, keepdims=True)
    shape = (adapters, index_row.shape[1])
    picked = jnp.where(iota(shape, 0) == index_row, column, 0.0)
    return jnp.sum(picked, axis=0, keepdims=True).astype(jnp.int32)


def owner_of(storage, holder, owners):
    owner = jnp.zeros_like(storage)
    for k in range(1, owners):
        owner = owner + (storage >= k * holder).astype(jnp.int32)
    return owner


def earlier(tokens):
    return one_hot(iota((tokens, tokens), 0) < iota((tokens, tokens), 1))


def routes(index_row, storage_row, holder, owners, group, first):
    tokens = index_row.shape[1]
    storage = storage_of(index_row, storage_row)
    owner = owner_of(storage, holder, owners)
    strict = earlier(tokens)
    rows = -(-owners // 8) * 8
    hits = iota((rows, tokens), 0) == owner
    rank = jnp.sum(jnp.where(hits, dot(one_hot(hits), strict), 0.0), axis=0, keepdims=True)
    late = jnp.where((owner != group) & (rank >= first), 1.0, 0.0)
    place = dot(jnp.broadcast_to(late, (8, tokens)).astype(BF16), strict)[0:1, :]
    late_place = jnp.where(late > 0, place, -1.0).astype(jnp.int32)
    return owner, storage, rank.astype(jnp.int32), late_place


def route_pack_kernel(owners, holder, first, pieces, me_ref, index_ref, storage_ref, tokens_ref, *refs):
    outs, dest_ref, pick = refs[: len(pieces)], refs[len(pieces)], refs[len(pieces) + 1]

    @pl.when(pl.program_id(0) == 0)
    def _():
        me = me_ref[0]
        owner, _, rank, late = routes(index_ref[...], storage_ref[...], holder, owners, me, first)
        away = owner - me
        away = jnp.where(away < 0, away + owners, away)
        dest = jnp.where(late >= 0, (owners - 1) * first + late, (away - 1) * first + rank)
        dest = jnp.where(away == 0, -1, dest)
        dest_ref[...] = dest
        pick[...] = one_hot(iota(pick.shape, 0) == dest)

    for (start, rows), out in zip(pieces, outs):
        out[...] = dot(pick[start : start + rows, :], tokens_ref[...]).astype(BF16)


def route_pack(me, index_row, storage_row, tokens, owners, holder, first, pieces):
    count, features = tokens.shape
    tile = features // 4 if features % 512 == 0 else features
    slots = max(start + rows for start, rows in pieces)
    return pl.pallas_call(
        functools.partial(route_pack_kernel, owners, holder, first, pieces),
        grid=(features // tile,),
        out_shape=[jax.ShapeDtypeStruct((rows, features), BF16) for _, rows in pieces]
        + [jax.ShapeDtypeStruct((1, count), jnp.int32)],
        in_specs=[
            IN_SMEM,
            pl.BlockSpec((1, count), lambda i: (0, 0)),
            pl.BlockSpec(storage_row.shape, lambda i: (0, 0)),
            pl.BlockSpec((count, tile), lambda i: (0, i)),
        ],
        out_specs=[pl.BlockSpec((rows, tile), lambda i: (0, i)) for _, rows in pieces]
        + [pl.BlockSpec((1, count), lambda i: (0, 0))],
        scratch_shapes=[pltpu.VMEM((slots, count), BF16)],
        compiler_params=params(),
        cost_estimate=CHEAP,
        name="route_pack",
    )(me, index_row, storage_row, tokens)


def arrivals_kernel(owners, holder, first, late, me_ref, storage_ref, *refs):
    index_refs = refs[:owners]
    ids_ref, late_ids_ref, home_ids_ref, more_ref = refs[owners:]
    tokens = index_refs[0].shape[1]
    me = me_ref[0]
    most = jnp.zeros((1, 1), jnp.int32)
    for shift in range(owners):
        group = lax.rem(me - shift + owners, owners)
        owner, storage, rank, place = routes(
            index_refs[shift][...], storage_ref[...], holder, owners, group, first
        )
        most = jnp.maximum(most, jnp.max(place, axis=1, keepdims=True))
        mine = owner == me
        local = jnp.where(mine, storage - me * holder, -1)
        if shift == 0:
            home_ids_ref[...] = local
            continue
        known = jnp.broadcast_to(jnp.where(mine, local + 1, 0).astype(F32), (8, tokens)).astype(BF16)
        slots = ids_ref.shape[1]
        pick = one_hot(iota((slots, tokens), 0) == jnp.where(mine & (place < 0), rank, -1))
        ids_ref[shift - 1 : shift, :] = dot(known, pick, ((1,), (1,)))[0:1, :].astype(jnp.int32) - 1
        slots = late_ids_ref.shape[1]
        pick = one_hot(iota((slots, tokens), 0) == jnp.where(mine, place, -1))
        late_ids_ref[shift - 1 : shift, :] = dot(known, pick, ((1,), (1,)))[0:1, :].astype(jnp.int32) - 1
    more_ref[0] = (jnp.max(most) >= late).astype(jnp.int32)


def arrivals(me, storage_row, index_rows, owners, holder, first, late):
    count = index_rows[0].shape[1]
    return pl.pallas_call(
        functools.partial(arrivals_kernel, owners, holder, first, late),
        out_shape=[
            jax.ShapeDtypeStruct((owners - 1, first), jnp.int32),
            jax.ShapeDtypeStruct((owners - 1, 2 * late), jnp.int32),
            jax.ShapeDtypeStruct((1, count), jnp.int32),
            jax.ShapeDtypeStruct((1,), jnp.int32),
        ],
        in_specs=[IN_SMEM] + [IN_VMEM] * (1 + owners),
        out_specs=[IN_VMEM, IN_VMEM, IN_VMEM, IN_SMEM],
        compiler_params=params(),
        cost_estimate=CHEAP,
        name="arrivals",
    )(me, storage_row, *index_rows)


def low_rank_kernel(blocks, copies, rank, ids_ref, down_ref, *refs):
    out = refs[-1]
    rows_refs = iter(refs)
    for k, ((row, start, rows, _), number) in enumerate(zip(blocks, copies)):
        rows_in = functools.reduce(jnp.add, [next(rows_refs)[...] for _ in range(number)])
        every = dot(down_ref[...], rows_in, ((1,), (1,)))
        ids = ids_ref[row : row + 1, start : start + rows]
        total = jnp.zeros((rank, rows), F32)
        for a in range(down_ref.shape[0] // rank):
            total = total + jnp.where(ids == a, every[a * rank : (a + 1) * rank, :], 0.0)
        out[k * rank : (k + 1) * rank, :] = total


def low_rank(ids, down, blocks, rows_in, rank):
    rows = blocks[0][2]
    copies = [len(x) for x in rows_in]
    return pl.pallas_call(
        functools.partial(low_rank_kernel, blocks, copies, rank),
        out_shape=jax.ShapeDtypeStruct((len(blocks) * rank, rows), F32),
        in_specs=[IN_VMEM] * (2 + sum(copies)),
        out_specs=IN_VMEM,
        compiler_params=params(),
        cost_estimate=CHEAP,
        name="low_rank",
    )(ids, down, *[x for group in rows_in for x in group])


def up_kernel(pieces, holder, rank, ids_ref, up_ref, a_ref, b_ref, *outs):
    up = up_ref[...]
    for k, ((row, start, rows), out) in enumerate(zip(pieces, outs)):
        own = slice(k * rank, (k + 1) * rank)
        ids = ids_ref[row : row + 1, start : start + rows]
        low = a_ref[own, :] + b_ref[own, :]
        spread = jnp.concatenate([jnp.where(ids == a, low, 0.0) for a in range(holder)], axis=0)
        high, rest = split_bf16(spread)
        out[...] = dot(high, up, ((0,), (0,))) + dot(rest, up, ((0,), (0,)))


def up_project(ids, up, pieces, a, b, holder):
    rank = up.shape[0] // holder
    return pl.pallas_call(
        functools.partial(up_kernel, pieces, holder, rank),
        out_shape=[jax.ShapeDtypeStruct((rows, up.shape[1]), F32) for _, _, rows in pieces],
        in_specs=[IN_VMEM] * 4,
        out_specs=[IN_VMEM] * len(pieces),
        compiler_params=params(),
        cost_estimate=CHEAP,
        name="up_project",
    )(ids, up, a, b)


def base_kernel(parts, me_ref, tokens_ref, value_ref, kept_ref, away_ref, full):
    width = full.shape[1] // parts
    full[...] = dot(tokens_ref[...], value_ref[...])
    for q in range(parts):
        block = me_ref[0] ^ q
        at = pl.ds(q // 2 * width, width)
        (away_ref if q % 2 else kept_ref)[:, at] = full[:, pl.ds(pl.multiple_of(block * width, width), width)]


def base_blocks(me, tokens, value, parts):
    count, columns = tokens.shape[0], value.shape[1]
    return pl.pallas_call(
        functools.partial(base_kernel, parts),
        out_shape=[jax.ShapeDtypeStruct((count, columns // 2), F32)] * 2,
        in_specs=[IN_SMEM, IN_VMEM, IN_VMEM],
        out_specs=[IN_VMEM, IN_VMEM],
        scratch_shapes=[pltpu.VMEM((count, columns), F32)],
        compiler_params=params(),
        cost_estimate=CHEAP,
        name="base_blocks",
    )(me, tokens, value)


def gather_add_kernel(pieces, terms, dest_ref, *refs):
    total = refs[0][...]
    for k in range(1, terms):
        total = total + refs[k][...]
    dest = dest_ref[...]
    returned = iter(refs[terms:])
    for start, rows, copies in pieces:
        piece = next(returned)[...]
        for _ in range(copies - 1):
            piece = piece + next(returned)[...]
        pick = one_hot(iota((rows, dest.shape[1]), 0) + start == dest)
        high, rest = split_bf16(ADAPTER_SCALE * piece)
        total = total + (dot(pick, high, ((0,), (0,))) + dot(pick, rest, ((0,), (0,))))
    refs[-1][...] = total.astype(refs[-1].dtype)


def gather_add(dest, pieces, terms, returned, dtype):
    return pl.pallas_call(
        functools.partial(gather_add_kernel, pieces, len(terms)),
        out_shape=jax.ShapeDtypeStruct(terms[0].shape, dtype),
        in_specs=[IN_VMEM] * (1 + len(terms) + len(returned)),
        out_specs=IN_VMEM,
        compiler_params=params(),
        cost_estimate=CHEAP,
        name="gather_add",
    )(dest, *terms, *returned)


def along(x, pairs):
    return lax.ppermute(x, "own", pairs)


def shifted(x, shift):
    size = lax.axis_size("own")
    return along(x, [(i, (i + shift) % size) for i in range(size)])


def beside(x):
    return shifted(x, 1), shifted(x, -1)


def opposite(before, after):
    return along(before, [(0, 1), (2, 3)]), along(after, [(1, 0), (3, 2)])


def partner(x, bit):
    return lax.ppermute(x, "tp", [(i, i ^ bit) for i in range(lax.axis_size("tp"))])


def two_terms(x):
    bit = 1
    while 2 * bit < lax.axis_size("tp"):
        x = x + partner(x, bit)
        bit *= 2
    return x, partner(x, bit)


def base_terms(me, tokens, value, parts):
    kept, away = base_blocks(me, tokens, value, parts)
    bit = 1
    while 2 * bit < parts:
        total = kept + partner(away, bit)
        blocks = jnp.split(total, parts // (2 * bit), axis=1)
        bit *= 2
        kept, away = (jnp.concatenate(blocks[k::2], axis=1) if len(blocks) > 2 else blocks[k] for k in range(2))
    return kept, partner(away, bit)


def direct(tokens, token_adapter_index, adapter_storage_row, value_matrix, down_stored, up_stored):
    owners, parts = lax.axis_size("own"), lax.axis_size("tp")
    count = tokens.shape[0]
    holder, _, rank = down_stored.shape
    cap = CAP * (2 * count // CAP // owners)
    first = cap * 5 // 8 // 16 * 16
    late = cap - first
    me = lax.axis_index("own").astype(jnp.int32).reshape(1)
    me_part = lax.axis_index("tp").astype(jnp.int32).reshape(1)
    index_row = token_adapter_index.reshape(1, count)
    storage_row = adapter_storage_row.reshape(1, -1)
    down = jnp.swapaxes(down_stored, 1, 2).reshape(holder * rank, -1)
    up = up_stored.reshape(holder * rank, -1)
    shifts = list(range(1, owners))
    late_start = (owners - 1) * first

    pieces = [((s - 1) * first, first) for s in shifts] + [(late_start + k * late, late) for k in range(2)]
    *packed, dest = route_pack(me, index_row, storage_row, tokens, owners, holder, first, pieces)
    index_rows = [index_row] + [shifted(index_row, s) for s in shifts]
    packed, index_rows = lax.optimization_barrier((packed, index_rows))
    before, after = beside(packed[owners - 1])
    rows_in = {s: shifted(packed[s - 1], s) for s in (1, 3, 2)}
    ids, late_ids, home_ids, more = arrivals(me, storage_row, index_rows, owners, holder, first, late)

    def terms(ids, blocks, rows_in):
        lows = two_terms(low_rank(ids, down, blocks, rows_in, rank))
        done = up_project(ids, up, [block[:3] for block in blocks], *lows, holder)
        return [x if block[3] is None else shifted(x, -block[3]) for block, x in zip(blocks, done)]

    base = base_terms(me_part, tokens, value_matrix, parts)
    (stays,) = terms(home_ids, [(0, 0, count, None)], [[tokens]])
    total = gather_add(dest, [], [*base, ADAPTER_SCALE * stays], [], F32)

    def late_terms(k, before, far, after):
        blocks = [(s - 1, k * late, late, s) for s in shifts]
        return terms(late_ids, blocks, [[before], list(far), [after]])

    def second(total, x):
        before, after = beside(x)
        back = late_terms(1, before, opposite(before, after), after)
        return gather_add(dest, [(late_start + late, late, owners - 1)], [total], back, F32)

    back = late_terms(0, before, opposite(before, after), after)
    total = gather_add(dest, [(late_start, late, owners - 1)], [total], back, F32)
    back = terms(ids, [(s - 1, 0, first, s) for s in (1, 3)], [[rows_in[1]], [rows_in[3]]])
    total = gather_add(dest, [((s - 1) * first, first, 1) for s in (1, 3)], [total], back, F32)
    total = lax.cond(more[0] > 0, second, lambda total, x: total, total, packed[owners])
    back = terms(ids, [(1, 0, first, 2)], [[rows_in[2]]])
    return gather_add(dest, [(first, first, 1)], [total], back, BF16)


def by_all_to_all(tokens, token_adapter_index, adapter_storage_row, value_matrix, down_stored, up_stored):
    owners = lax.axis_size("own")
    tok_dev, features = tokens.shape
    holder, _, rank = down_stored.shape
    cap = CAP * (2 * tok_dev // CAP // owners)
    slots = owners * cap
    catalog = jnp.arange(adapter_storage_row.shape[0], dtype=jnp.int32)
    storage = jnp.sum(
        jnp.where(token_adapter_index[:, None] == catalog[None, :], adapter_storage_row[None, :], 0), axis=1
    )
    home_owner = storage // holder
    hits = (home_owner[:, None] == jnp.arange(owners, dtype=jnp.int32)[None, :]).astype(jnp.int32)
    before = jnp.cumsum(hits, axis=0) - hits
    dest = home_owner * cap + jnp.sum(before * hits, axis=1)
    outgoing = jnp.zeros((slots, features), tokens.dtype).at[dest].set(tokens)
    which = jnp.full((slots,), holder, jnp.int32).at[dest].set(storage % holder)
    base = jnp.dot(tokens, value_matrix, preferred_element_type=F32)
    rows_in = lax.all_to_all(
        outgoing.reshape(owners, cap, features), "own", split_axis=0, concat_axis=0, tiled=True
    ).reshape(slots, features)
    which = lax.all_to_all(which.reshape(owners, cap), "own", split_axis=0, concat_axis=0, tiled=True)
    selector = (which.reshape(slots)[:, None] == jnp.arange(holder)[None, :]).astype(F32)
    every = jnp.einsum("nf,afr->nar", rows_in, down_stored, preferred_element_type=F32)
    low = lax.psum(jnp.sum(every * selector[:, :, None], axis=1), "tp")
    spread = (selector[:, :, None] * low[:, None, :]).reshape(slots, holder * rank)
    stacked = up_stored.reshape(holder * rank, -1).astype(F32)
    term = jnp.dot(spread, stacked, precision=lax.Precision.HIGHEST).reshape(owners, cap, -1)
    term = lax.all_to_all(term, "own", split_axis=0, concat_axis=0, tiled=True).reshape(slots, -1)[dest]
    mixed = lax.psum_scatter(base, "tp", scatter_dimension=1, tiled=True) + ADAPTER_SCALE * term
    return mixed.astype(BF16)


def solution(mesh):
    owners, parts = mesh.shape["own"], mesh.shape["tp"]
    on_a_line = owners == LINE and parts > 1 and parts & (parts - 1) == 0
    body = direct if on_a_line else by_all_to_all
    return jax.shard_map(
        body,
        mesh=mesh,
        in_specs=(
            P(("rep", "own"), "tp"),
            P(("rep", "own")),
            P("rep"),
            P("tp", None),
            P(("rep", "own"), "tp", None),
            P(("rep", "own"), None, "tp"),
        ),
        out_specs=P(("rep", "own"), "tp"),
        check_vma=False,
    )
```

```python
import functools

import jax
import jax.numpy as jnp
from jax import lax
from jax.experimental import pallas as pl
from jax.experimental.pallas import tpu as pltpu
from jax.sharding import PartitionSpec as P

CAP = 4
ADAPTER_SCALE = 0.5
LINE = 4
BF16 = jnp.bfloat16
F32 = jnp.float32
VMEM_LIMIT = 16 * 2**20
CHEAP = pl.CostEstimate(flops=1, bytes_accessed=1, transcendentals=0)


def params(**kw):
    return pltpu.CompilerParams(vmem_limit_bytes=VMEM_LIMIT, **kw)


def iota(shape, dim):
    return lax.broadcasted_iota(jnp.int32, shape, dim)


def dot(a, b, dims=((1,), (0,))):
    return lax.dot_general(a, b, (dims, ((), ())), preferred_element_type=F32)


def split_bf16(x):
    high = x.astype(BF16)
    return high, (x - high.astype(F32)).astype(BF16)


def one_hot(mask):
    return mask.astype(F32).astype(BF16)


IN_VMEM = pl.BlockSpec(memory_space=pltpu.VMEM)
IN_SMEM = pl.BlockSpec(memory_space=pltpu.SMEM)


def storage_of(index_row, storage_row):
    adapters = storage_row.shape[1]
    square = (adapters, adapters)
    diagonal = jnp.where(iota(square, 0) == iota(square, 1), storage_row.astype(F32), 0.0)
    column = jnp.sum(diagonal, axis=1, keepdims=True)
    shape = (adapters, index_row.shape[1])
    picked = jnp.where(iota(shape, 0) == index_row, column, 0.0)
    return jnp.sum(picked, axis=0, keepdims=True).astype(jnp.int32)


def owner_of(storage, holder, owners):
    owner = jnp.zeros_like(storage)
    for k in range(1, owners):
        owner = owner + (storage >= k * holder).astype(jnp.int32)
    return owner


def earlier(tokens):
    return one_hot(iota((tokens, tokens), 0) < iota((tokens, tokens), 1))


def routes(index_row, storage_row, holder, owners, group, first):
    tokens = index_row.shape[1]
    storage = storage_of(index_row, storage_row)
    owner = owner_of(storage, holder, owners)
    strict = earlier(tokens)
    rows = -(-owners // 8) * 8
    hits = iota((rows, tokens), 0) == owner
    rank = jnp.sum(jnp.where(hits, dot(one_hot(hits), strict), 0.0), axis=0, keepdims=True)
    late = jnp.where((owner != group) & (rank >= first), 1.0, 0.0)
    place = dot(jnp.broadcast_to(late, (8, tokens)).astype(BF16), strict)[0:1, :]
    late_place = jnp.where(late > 0, place, -1.0).astype(jnp.int32)
    return owner, storage, rank.astype(jnp.int32), late_place


def route_pack_kernel(owners, holder, first, pieces, me_ref, index_hbm, storage_hbm, tokens_hbm, *refs):
    outs, (dest_ref, pick, index, storage, tokens, sems) = refs[: len(pieces)], refs[len(pieces) :]
    tiles = tokens.shape[0]
    tile = tokens.shape[2]
    small = [pltpu.make_async_copy(index_hbm, index, sems.at[tiles])]
    small += [pltpu.make_async_copy(storage_hbm, storage, sems.at[tiles + 1])]
    large = [
        pltpu.make_async_copy(tokens_hbm.at[:, pl.ds(i * tile, tile)], tokens.at[i], sems.at[i])
        for i in range(tiles)
    ]
    for copy in small + large:
        copy.start()
    for copy in small:
        copy.wait()
    me = me_ref[0]
    owner, _, rank, late = routes(index[...], storage[...], holder, owners, me, first)
    away = owner - me
    away = jnp.where(away < 0, away + owners, away)
    dest = jnp.where(late >= 0, (owners - 1) * first + late, (away - 1) * first + rank)
    dest = jnp.where(away == 0, -1, dest)
    dest_ref[...] = dest
    pick[...] = one_hot(iota(pick.shape, 0) == dest)
    for i, copy in enumerate(large):
        copy.wait()
        for ranges, out in zip(pieces, outs):
            at = 0
            for start, rows in ranges:
                out[at : at + rows, i * tile : (i + 1) * tile] = dot(
                    pick[start : start + rows, :], tokens[i]
                ).astype(BF16)
                at += rows


def route_pack(me, index_row, storage_row, tokens, owners, holder, first, pieces):
    count, features = tokens.shape
    tiles = 4 if features % 512 == 0 else 1
    slots = max(start + rows for ranges in pieces for start, rows in ranges)
    in_hbm = pl.BlockSpec(memory_space=pltpu.HBM)
    return pl.pallas_call(
        functools.partial(route_pack_kernel, owners, holder, first, pieces),
        out_shape=[jax.ShapeDtypeStruct((sum(r for _, r in ranges), features), BF16) for ranges in pieces]
        + [jax.ShapeDtypeStruct((1, count), jnp.int32)],
        in_specs=[IN_SMEM, in_hbm, in_hbm, in_hbm],
        out_specs=[IN_VMEM] * (len(pieces) + 1),
        scratch_shapes=[
            pltpu.VMEM((slots, count), BF16),
            pltpu.VMEM(index_row.shape, jnp.int32),
            pltpu.VMEM(storage_row.shape, jnp.int32),
            pltpu.VMEM((tiles, count, features // tiles), BF16),
            pltpu.SemaphoreType.DMA((tiles + 2,)),
        ],
        compiler_params=params(),
        cost_estimate=CHEAP,
        name="route_pack",
    )(me, index_row, storage_row, tokens)


def repack_kernel(start, dest_ref, tokens_ref, out):
    pick = one_hot(iota((out.shape[0], dest_ref.shape[1]), 0) + start == dest_ref[...])
    out[...] = dot(pick, tokens_ref[...]).astype(BF16)


def repack(dest, tokens, start, rows):
    return pl.pallas_call(
        functools.partial(repack_kernel, start),
        out_shape=jax.ShapeDtypeStruct((rows, tokens.shape[1]), BF16),
        in_specs=[IN_VMEM] * 2,
        out_specs=IN_VMEM,
        compiler_params=params(),
        name="repack",
    )(dest, tokens)


def arrivals_kernel(owners, holder, first, late, me_ref, storage_ref, *refs):
    index_refs = refs[:owners]
    ids_ref, home_ids_ref, more_ref = refs[owners:]
    tokens = index_refs[0].shape[1]
    me = me_ref[0]
    most = jnp.zeros((1, 1), jnp.int32)
    for shift in range(owners):
        group = lax.rem(me - shift + owners, owners)
        owner, storage, rank, place = routes(
            index_refs[shift][...], storage_ref[...], holder, owners, group, first
        )
        most = jnp.maximum(most, jnp.max(place, axis=1, keepdims=True))
        mine = owner == me
        local = jnp.where(mine, storage - me * holder, -1)
        if shift == 0:
            home_ids_ref[...] = local
            continue
        known = jnp.broadcast_to(jnp.where(mine, local + 1, 0).astype(F32), (8, tokens)).astype(BF16)
        slot = jnp.where(place >= 0, first + place, rank)
        pick = one_hot(iota((ids_ref.shape[1], tokens), 0) == jnp.where(mine, slot, -1))
        ids_ref[shift - 1 : shift, :] = dot(known, pick, ((1,), (1,)))[0:1, :].astype(jnp.int32) - 1
    more_ref[0] = (jnp.max(most) >= late).astype(jnp.int32)


def arrivals(me, storage_row, index_rows, owners, holder, first, late):
    count = index_rows[0].shape[1]
    return pl.pallas_call(
        functools.partial(arrivals_kernel, owners, holder, first, late),
        out_shape=[
            jax.ShapeDtypeStruct((owners - 1, first + 2 * late), jnp.int32),
            jax.ShapeDtypeStruct((1, count), jnp.int32),
            jax.ShapeDtypeStruct((1,), jnp.int32),
        ],
        in_specs=[IN_SMEM] + [IN_VMEM] * (1 + owners),
        out_specs=[IN_VMEM, IN_VMEM, IN_SMEM],
        compiler_params=params(),
        cost_estimate=CHEAP,
        name="arrivals",
    )(me, storage_row, *index_rows)


def low_rank_kernel(blocks, copies, rank, ids_ref, down_ref, *refs):
    out = refs[-1]
    rows_refs = iter(refs)
    for k, ((row, start, rows, _), number) in enumerate(zip(blocks, copies)):
        rows_in = functools.reduce(jnp.add, [next(rows_refs)[...] for _ in range(number)])
        every = dot(down_ref[...], rows_in, ((1,), (1,)))
        ids = ids_ref[row : row + 1, start : start + rows]
        total = jnp.zeros((rank, rows), F32)
        for a in range(down_ref.shape[0] // rank):
            total = total + jnp.where(ids == a, every[a * rank : (a + 1) * rank, :], 0.0)
        out[k * rank : (k + 1) * rank, :] = total


def low_rank(ids, down, blocks, rows_in, rank):
    rows = blocks[0][2]
    copies = [len(x) for x in rows_in]
    return pl.pallas_call(
        functools.partial(low_rank_kernel, blocks, copies, rank),
        out_shape=jax.ShapeDtypeStruct((len(blocks) * rank, rows), F32),
        in_specs=[IN_VMEM] * (2 + sum(copies)),
        out_specs=IN_VMEM,
        compiler_params=params(),
        cost_estimate=CHEAP,
        name="low_rank",
    )(ids, down, *[x for group in rows_in for x in group])


def up_kernel(pieces, holder, rank, ids_ref, up_ref, a_ref, b_ref, *outs):
    up = up_ref[...]
    for k, ((row, start, rows), out) in enumerate(zip(pieces, outs)):
        own = slice(k * rank, (k + 1) * rank)
        ids = ids_ref[row : row + 1, start : start + rows]
        low = a_ref[own, :] + b_ref[own, :]
        spread = jnp.concatenate([jnp.where(ids == a, low, 0.0) for a in range(holder)], axis=0)
        high, rest = split_bf16(spread)
        out[...] = dot(high, up, ((0,), (0,))) + dot(rest, up, ((0,), (0,)))


def up_project(ids, up, pieces, a, b, holder):
    rank = up.shape[0] // holder
    return pl.pallas_call(
        functools.partial(up_kernel, pieces, holder, rank),
        out_shape=[jax.ShapeDtypeStruct((rows, up.shape[1]), F32) for _, _, rows in pieces],
        in_specs=[IN_VMEM] * 4,
        out_specs=[IN_VMEM] * len(pieces),
        compiler_params=params(),
        cost_estimate=CHEAP,
        name="up_project",
    )(ids, up, a, b)


def base_kernel(parts, me_ref, tokens_ref, value_ref, kept_ref, away_ref, full):
    width = full.shape[1] // parts
    full[...] = dot(tokens_ref[...], value_ref[...])
    for q in range(parts):
        block = me_ref[0] ^ q
        at = pl.ds(q // 2 * width, width)
        (away_ref if q % 2 else kept_ref)[:, at] = full[:, pl.ds(pl.multiple_of(block * width, width), width)]


def base_blocks(me, tokens, value, parts):
    count, columns = tokens.shape[0], value.shape[1]
    return pl.pallas_call(
        functools.partial(base_kernel, parts),
        out_shape=[jax.ShapeDtypeStruct((count, columns // 2), F32)] * 2,
        in_specs=[IN_SMEM, IN_VMEM, IN_VMEM],
        out_specs=[IN_VMEM, IN_VMEM],
        scratch_shapes=[pltpu.VMEM((count, columns), F32)],
        compiler_params=params(),
        cost_estimate=CHEAP,
        name="base_blocks",
    )(me, tokens, value)


def gather_add_kernel(pieces, terms, dest_ref, *refs):
    total = refs[0][...]
    for k in range(1, terms):
        total = total + refs[k][...]
    dest = dest_ref[...]
    for start, rows, sources in pieces:
        piece = functools.reduce(jnp.add, [refs[terms + j][at : at + rows, :] for j, at in sources])
        pick = one_hot(iota((rows, dest.shape[1]), 0) + start == dest)
        high, rest = split_bf16(ADAPTER_SCALE * piece)
        total = total + (dot(pick, high, ((0,), (0,))) + dot(pick, rest, ((0,), (0,))))
    refs[-1][...] = total.astype(refs[-1].dtype)


def gather_add(dest, pieces, terms, returned, dtype):
    return pl.pallas_call(
        functools.partial(gather_add_kernel, pieces, len(terms)),
        out_shape=jax.ShapeDtypeStruct(terms[0].shape, dtype),
        in_specs=[IN_VMEM] * (1 + len(terms) + len(returned)),
        out_specs=IN_VMEM,
        compiler_params=params(),
        cost_estimate=CHEAP,
        name="gather_add",
    )(dest, *terms, *returned)


def along(x, pairs):
    return lax.ppermute(x, "own", pairs)


def shifted(x, shift):
    size = lax.axis_size("own")
    return along(x, [(i, (i + shift) % size) for i in range(size)])


def opposite(before, after):
    return along(before, [(0, 1), (2, 3)]), along(after, [(1, 0), (3, 2)])


def partner(x, bit):
    return lax.ppermute(x, "tp", [(i, i ^ bit) for i in range(lax.axis_size("tp"))])


def two_terms(x):
    bit = 1
    while 2 * bit < lax.axis_size("tp"):
        x = x + partner(x, bit)
        bit *= 2
    return x, partner(x, bit)


def base_terms(me, tokens, value, parts):
    kept, away = base_blocks(me, tokens, value, parts)
    bit = 1
    while 2 * bit < parts:
        total = kept + partner(away, bit)
        blocks = jnp.split(total, parts // (2 * bit), axis=1)
        bit *= 2
        kept, away = (jnp.concatenate(blocks[k::2], axis=1) if len(blocks) > 2 else blocks[k] for k in range(2))
    return kept, partner(away, bit)


def direct(tokens, token_adapter_index, adapter_storage_row, value_matrix, down_stored, up_stored):
    owners, parts = lax.axis_size("own"), lax.axis_size("tp")
    count = tokens.shape[0]
    holder, _, rank = down_stored.shape
    cap = CAP * (2 * count // CAP // owners)
    first = cap * 5 // 8 // 16 * 16
    late = cap - first
    me = lax.axis_index("own").astype(jnp.int32).reshape(1)
    me_part = lax.axis_index("tp").astype(jnp.int32).reshape(1)
    index_row = token_adapter_index.reshape(1, count)
    storage_row = adapter_storage_row.reshape(1, -1)
    down = jnp.swapaxes(down_stored, 1, 2).reshape(holder * rank, -1)
    up = up_stored.reshape(holder * rank, -1)
    shifts = list(range(1, owners))
    late_start = (owners - 1) * first

    mains = {s: ((s - 1) * first, first) for s in shifts}
    pieces = [[mains[1], (late_start, late)], [mains[2]], [mains[3], (late_start, late)]]
    *packed, dest = route_pack(me, index_row, storage_row, tokens, owners, holder, first, pieces)
    index_rows = [index_row] + [shifted(index_row, s) for s in shifts]
    packed, index_rows = lax.optimization_barrier((packed, index_rows))
    below, above, across = (shifted(packed[s - 1], s) for s in (1, 3, 2))
    ids, home_ids, more = arrivals(me, storage_row, index_rows, owners, holder, first, late)

    def terms(ids, blocks, rows_in):
        lows = two_terms(low_rank(ids, down, blocks, rows_in, rank))
        done = up_project(ids, up, [block[:3] for block in blocks], *lows, holder)
        return [x if block[3] is None else shifted(x, -block[3]) for block, x in zip(blocks, done)]

    def second(total):
        x = repack(dest, tokens, late_start + late, late)
        below, above = shifted(x, 1), shifted(x, 3)
        blocks = [(s - 1, first + late, late, s) for s in shifts]
        back = terms(ids, blocks, [[below], list(opposite(below, above)), [above]])
        return gather_add(dest, [(late_start + late, late, [(j, 0) for j in range(3)])], [total], back, F32)

    base = base_terms(me_part, tokens, value_matrix, parts)
    (stays,) = terms(home_ids, [(0, 0, count, None)], [[tokens]])
    total = gather_add(dest, [], [*base, ADAPTER_SCALE * stays], [], F32)
    below, above, total = lax.optimization_barrier((below, above, total))
    passed = opposite(below[first:], above[first:])
    back = terms(ids, [(s - 1, 0, first + late, s) for s in (1, 3)], [[below], [above]])
    pieces = [(*mains[1], [(0, 0)]), (*mains[3], [(1, 0)]), (late_start, late, [(0, first), (1, first)])]
    total = gather_add(dest, pieces, [total], back, F32)
    back = terms(ids, [(1, first, late, 2)], [list(passed)])
    total = gather_add(dest, [(late_start, late, [(0, 0)])], [total], back, F32)
    total = lax.cond(more[0] > 0, second, lambda total: total, total)
    back = terms(ids, [(1, 0, first, 2)], [[across]])
    return gather_add(dest, [(*mains[2], [(0, 0)])], [total], back, BF16)


def by_all_to_all(tokens, token_adapter_index, adapter_storage_row, value_matrix, down_stored, up_stored):
    owners = lax.axis_size("own")
    tok_dev, features = tokens.shape
    holder, _, rank = down_stored.shape
    cap = CAP * (2 * tok_dev // CAP // owners)
    slots = owners * cap
    catalog = jnp.arange(adapter_storage_row.shape[0], dtype=jnp.int32)
    storage = jnp.sum(
        jnp.where(token_adapter_index[:, None] == catalog[None, :], adapter_storage_row[None, :], 0), axis=1
    )
    home_owner = storage // holder
    hits = (home_owner[:, None] == jnp.arange(owners, dtype=jnp.int32)[None, :]).astype(jnp.int32)
    before = jnp.cumsum(hits, axis=0) - hits
    dest = home_owner * cap + jnp.sum(before * hits, axis=1)
    outgoing = jnp.zeros((slots, features), tokens.dtype).at[dest].set(tokens)
    which = jnp.full((slots,), holder, jnp.int32).at[dest].set(storage % holder)
    base = jnp.dot(tokens, value_matrix, preferred_element_type=F32)
    rows_in = lax.all_to_all(
        outgoing.reshape(owners, cap, features), "own", split_axis=0, concat_axis=0, tiled=True
    ).reshape(slots, features)
    which = lax.all_to_all(which.reshape(owners, cap), "own", split_axis=0, concat_axis=0, tiled=True)
    selector = (which.reshape(slots)[:, None] == jnp.arange(holder)[None, :]).astype(F32)
    every = jnp.einsum("nf,afr->nar", rows_in, down_stored, preferred_element_type=F32)
    low = lax.psum(jnp.sum(every * selector[:, :, None], axis=1), "tp")
    spread = (selector[:, :, None] * low[:, None, :]).reshape(slots, holder * rank)
    stacked = up_stored.reshape(holder * rank, -1).astype(F32)
    term = jnp.dot(spread, stacked, precision=lax.Precision.HIGHEST).reshape(owners, cap, -1)
    term = lax.all_to_all(term, "own", split_axis=0, concat_axis=0, tiled=True).reshape(slots, -1)[dest]
    mixed = lax.psum_scatter(base, "tp", scatter_dimension=1, tiled=True) + ADAPTER_SCALE * term
    return mixed.astype(BF16)


def solution(mesh):
    owners, parts = mesh.shape["own"], mesh.shape["tp"]
    on_a_line = owners == LINE and parts > 1 and parts & (parts - 1) == 0
    body = direct if on_a_line else by_all_to_all
    return jax.shard_map(
        body,
        mesh=mesh,
        in_specs=(
            P(("rep", "own"), "tp"),
            P(("rep", "own")),
            P("rep"),
            P("tp", None),
            P(("rep", "own"), "tp", None),
            P(("rep", "own"), None, "tp"),
        ),
        out_specs=P(("rep", "own"), "tp"),
        check_vma=False,
    )
```

```python
import functools

import jax
import jax.numpy as jnp
from jax import lax
from jax.experimental import pallas as pl
from jax.experimental.pallas import tpu as pltpu
from jax.sharding import PartitionSpec as P

CAP = 4
ADAPTER_SCALE = 0.5
TAGS = 16
LINE = 4
BF16 = jnp.bfloat16
F32 = jnp.float32
VMEM_LIMIT = 16 * 2**20
CHEAP = pl.CostEstimate(flops=1, bytes_accessed=1, transcendentals=0)


def params(**kw):
    return pltpu.CompilerParams(vmem_limit_bytes=VMEM_LIMIT, **kw)


def iota(shape, dim):
    return lax.broadcasted_iota(jnp.int32, shape, dim)


def dot(a, b, dims=((1,), (0,))):
    return lax.dot_general(a, b, (dims, ((), ())), preferred_element_type=F32)


def split_bf16(x):
    high = x.astype(BF16)
    return high, (x - high.astype(F32)).astype(BF16)


def one_hot(mask):
    return mask.astype(F32).astype(BF16)


IN_VMEM = pl.BlockSpec(memory_space=pltpu.VMEM)
IN_SMEM = pl.BlockSpec(memory_space=pltpu.SMEM)


def storage_of(index_row, storage_row):
    adapters = storage_row.shape[1]
    square = (adapters, adapters)
    diagonal = jnp.where(iota(square, 0) == iota(square, 1), storage_row.astype(F32), 0.0)
    column = jnp.sum(diagonal, axis=1, keepdims=True)
    shape = (adapters, index_row.shape[1])
    picked = jnp.where(iota(shape, 0) == index_row, column, 0.0)
    return jnp.sum(picked, axis=0, keepdims=True).astype(jnp.int32)


def owner_of(storage, holder, owners):
    owner = jnp.zeros_like(storage)
    for k in range(1, owners):
        owner = owner + (storage >= k * holder).astype(jnp.int32)
    return owner


def earlier(tokens):
    return one_hot(iota((tokens, tokens), 0) < iota((tokens, tokens), 1))


def routes(index_row, storage_row, holder, owners, group, first):
    tokens = index_row.shape[1]
    storage = storage_of(index_row, storage_row)
    owner = owner_of(storage, holder, owners)
    strict = earlier(tokens)
    rows = -(-owners // 8) * 8
    hits = iota((rows, tokens), 0) == owner
    rank = jnp.sum(jnp.where(hits, dot(one_hot(hits), strict), 0.0), axis=0, keepdims=True)
    late = jnp.where((owner != group) & (rank >= first), 1.0, 0.0)
    place = dot(jnp.broadcast_to(late, (8, tokens)).astype(BF16), strict)[0:1, :]
    late_place = jnp.where(late > 0, place, -1.0).astype(jnp.int32)
    return owner, storage, rank.astype(jnp.int32), late_place


def known_adapters(storage, picks, flag):
    tokens = storage.shape[1]
    known = jnp.broadcast_to((storage + 1).astype(F32), (8, tokens)).astype(BF16)
    width = picks[0].shape[0]
    which = iota((TAGS, width), 0)
    tags = jnp.where(which == TAGS - 1, flag, 0.0)
    for k, pick in enumerate(picks):
        row = dot(known, pick, ((1,), (1,)))
        tags = jnp.where(which == k, jnp.concatenate([row] * (TAGS // 8), axis=0), tags)
    return tags.astype(BF16)


def route_pack_kernel(owners, holder, first, late, me_ref, index_hbm, storage_hbm, tokens_hbm, *refs):
    outs, (dest_ref, home_ids_ref, more_ref, picks, index, storage, tokens, sems) = refs[:3], refs[3:]
    tiles, _, tile = tokens.shape
    small = [pltpu.make_async_copy(index_hbm, index, sems.at[tiles])]
    small += [pltpu.make_async_copy(storage_hbm, storage, sems.at[tiles + 1])]
    large = [
        pltpu.make_async_copy(tokens_hbm.at[:, pl.ds(i * tile, tile)], tokens.at[i], sems.at[i])
        for i in range(tiles)
    ]
    for copy in small + large:
        copy.start()
    for copy in small:
        copy.wait()
    me = me_ref[0]
    owner, row, rank, place = routes(index[...], storage[...], holder, owners, me, first)
    home_ids_ref[...] = jnp.where(owner == me, row - me * holder, -1)
    away = owner - me
    away = jnp.where(away < 0, away + owners, away)
    dest = jnp.where(place >= 0, (owners - 1) * first + place, (away - 1) * first + rank)
    dest_ref[...] = jnp.where(away == 0, -1, dest)
    more = (jnp.max(place) >= late).astype(jnp.int32)
    more_ref[0] = more
    for s in range(1, owners):
        slot = jnp.where(place >= 0, first + place, jnp.where(away == s, rank, -1))
        picks[s - 1] = one_hot(iota(picks.shape[1:], 0) == slot)
    tags = known_adapters(row, [picks[s - 1] for s in range(1, owners)], more.astype(F32))
    size = first + late
    for out in (outs[0], outs[2]):
        out[size:, :] = jnp.zeros((TAGS, out.shape[1]), BF16)
        out[size:, 0:size] = tags
    for i, copy in enumerate(large):
        copy.wait()
        at = slice(i * tile, (i + 1) * tile)
        for s, rows in ((1, size), (3, first), (2, first)):
            if s == 3:
                outs[2][0:first, at] = dot(picks[2, 0:first, :], tokens[i]).astype(BF16)
                outs[2][first:size, at] = outs[0][first:size, at]
            else:
                outs[s - 1][0:rows, at] = dot(picks[s - 1, 0:rows, :], tokens[i]).astype(BF16)


def route_pack(me, index_row, storage_row, tokens, owners, holder, first, late):
    count, features = tokens.shape
    tiles = 4 if features % 512 == 0 else 1
    in_hbm = pl.BlockSpec(memory_space=pltpu.HBM)
    long = first + late + TAGS
    return pl.pallas_call(
        functools.partial(route_pack_kernel, owners, holder, first, late),
        out_shape=[jax.ShapeDtypeStruct((rows, features), BF16) for rows in (long, first, long)]
        + [jax.ShapeDtypeStruct((1, count), jnp.int32)] * 2
        + [jax.ShapeDtypeStruct((1,), jnp.int32)],
        in_specs=[IN_SMEM, in_hbm, in_hbm, in_hbm],
        out_specs=[IN_VMEM] * 5 + [IN_SMEM],
        scratch_shapes=[
            pltpu.VMEM((owners - 1, first + late, count), BF16),
            pltpu.VMEM(index_row.shape, jnp.int32),
            pltpu.VMEM(storage_row.shape, jnp.int32),
            pltpu.VMEM((tiles, count, features // tiles), BF16),
            pltpu.SemaphoreType.DMA((tiles + 2,)),
        ],
        compiler_params=params(),
        cost_estimate=CHEAP,
        name="route_pack",
    )(me, index_row, storage_row, tokens)


def repack_kernel(start, index_ref, storage_ref, dest_ref, tokens_ref, out):
    rows = out.shape[0] - TAGS
    pick = one_hot(iota((rows, dest_ref.shape[1]), 0) + start == dest_ref[...])
    out[0:rows, :] = dot(pick, tokens_ref[...]).astype(BF16)
    out[rows:, :] = jnp.zeros((TAGS, out.shape[1]), BF16)
    out[rows:, 0:rows] = known_adapters(storage_of(index_ref[...], storage_ref[...]), [pick], 0.0)


def repack(index_row, storage_row, dest, tokens, start, rows):
    return pl.pallas_call(
        functools.partial(repack_kernel, start),
        out_shape=jax.ShapeDtypeStruct((rows + TAGS, tokens.shape[1]), BF16),
        in_specs=[IN_VMEM] * 4,
        out_specs=IN_VMEM,
        compiler_params=params(),
        name="repack",
    )(index_row, storage_row, dest, tokens)


def low_rank_kernel(blocks, joined, holder, rank, me_ref, down_ref, *refs):
    out, ids_out, flag = refs[-3:]
    lead = me_ref[0] * holder + 1
    flags = jnp.zeros((1, 1), F32)
    for k, (rows, sources, tagged, row, tag_start) in enumerate(blocks):
        rows_in = functools.reduce(jnp.add, [refs[j][at : at + rows, :] for j, at in sources])
        every = dot(down_ref[...], rows_in, ((1,), (1,)))
        tags = functools.reduce(jnp.add, [refs[j][at : at + TAGS, :].astype(F32) for j, at in tagged])
        flags = jnp.maximum(flags, tags[TAGS - 1 : TAGS, 0:1])
        ids = tags[row : row + 1, tag_start : tag_start + rows].astype(jnp.int32) - lead
        total = jnp.zeros((rank, rows), F32)
        for a in range(holder):
            total = total + jnp.where(ids == a, every[a * rank : (a + 1) * rank, :], 0.0)
        at = slice(tag_start, tag_start + rows)
        if joined:
            out[:, at] = total
            ids_out[:, at] = ids
        else:
            out[k * rank : (k + 1) * rank, :] = total
            ids_out[k : k + 1, :] = ids
    flag[0] = jnp.max(flags).astype(jnp.int32)


def low_rank(me, down, blocks, messages, holder, joined=False):
    rank = down.shape[0] // holder
    rows = sum(block[0] for block in blocks) if joined else blocks[0][0]
    number = 1 if joined else len(blocks)
    return pl.pallas_call(
        functools.partial(low_rank_kernel, blocks, joined, holder, rank),
        out_shape=[
            jax.ShapeDtypeStruct((number * rank, rows), F32),
            jax.ShapeDtypeStruct((number, rows), jnp.int32),
            jax.ShapeDtypeStruct((1,), jnp.int32),
        ],
        in_specs=[IN_SMEM] + [IN_VMEM] * (1 + len(messages)),
        out_specs=[IN_VMEM, IN_VMEM, IN_SMEM],
        compiler_params=params(),
        cost_estimate=CHEAP,
        name="low_rank",
    )(me, down, *messages)


def low_rank_home_kernel(holder, rank, ids_ref, down_ref, tokens_ref, out):
    every = dot(down_ref[...], tokens_ref[...], ((1,), (1,)))
    ids = ids_ref[...]
    total = jnp.zeros(out.shape, F32)
    for a in range(holder):
        total = total + jnp.where(ids == a, every[a * rank : (a + 1) * rank, :], 0.0)
    out[...] = total


def low_rank_home(ids, down, tokens, holder):
    rank = down.shape[0] // holder
    return pl.pallas_call(
        functools.partial(low_rank_home_kernel, holder, rank),
        out_shape=jax.ShapeDtypeStruct((rank, tokens.shape[0]), F32),
        in_specs=[IN_VMEM] * 3,
        out_specs=IN_VMEM,
        compiler_params=params(),
        cost_estimate=CHEAP,
        name="low_rank_home",
    )(ids, down, tokens)


def up_kernel(rows, holder, rank, ids_ref, up_ref, a_ref, b_ref, *outs):
    up = up_ref[...]
    for k, out in enumerate(outs):
        own = slice(k * rank, (k + 1) * rank)
        low = a_ref[own, :] + b_ref[own, :]
        ids = ids_ref[k : k + 1, :]
        spread = jnp.concatenate([jnp.where(ids == a, low, 0.0) for a in range(holder)], axis=0)
        high, rest = split_bf16(spread)
        out[...] = dot(high, up, ((0,), (0,))) + dot(rest, up, ((0,), (0,)))


def up_project(ids, up, a, b, holder):
    blocks, rows = ids.shape
    rank = up.shape[0] // holder
    return pl.pallas_call(
        functools.partial(up_kernel, rows, holder, rank),
        out_shape=[jax.ShapeDtypeStruct((rows, up.shape[1]), F32)] * blocks,
        in_specs=[IN_VMEM] * 4,
        out_specs=[IN_VMEM] * blocks,
        compiler_params=params(),
        cost_estimate=CHEAP,
        name="up_project",
    )(ids, up, a, b)


def base_kernel(parts, me_ref, tokens_ref, value_ref, kept_ref, away_ref, full):
    width = full.shape[1] // parts
    full[...] = dot(tokens_ref[...], value_ref[...])
    for q in range(parts):
        block = me_ref[0] ^ q
        at = pl.ds(q // 2 * width, width)
        (away_ref if q % 2 else kept_ref)[:, at] = full[:, pl.ds(pl.multiple_of(block * width, width), width)]


def base_blocks(me, tokens, value, parts):
    count, columns = tokens.shape[0], value.shape[1]
    return pl.pallas_call(
        functools.partial(base_kernel, parts),
        out_shape=[jax.ShapeDtypeStruct((count, columns // 2), F32)] * 2,
        in_specs=[IN_SMEM, IN_VMEM, IN_VMEM],
        out_specs=[IN_VMEM, IN_VMEM],
        scratch_shapes=[pltpu.VMEM((count, columns), F32)],
        compiler_params=params(),
        cost_estimate=CHEAP,
        name="base_blocks",
    )(me, tokens, value)


def gather_add_kernel(pieces, terms, dest_ref, *refs):
    total = refs[0][...]
    for k in range(1, terms):
        total = total + refs[k][...]
    dest = dest_ref[...]
    for start, rows, sources in pieces:
        piece = functools.reduce(jnp.add, [refs[terms + j][at : at + rows, :] for j, at in sources])
        pick = one_hot(iota((rows, dest.shape[1]), 0) + start == dest)
        high, rest = split_bf16(ADAPTER_SCALE * piece)
        total = total + (dot(pick, high, ((0,), (0,))) + dot(pick, rest, ((0,), (0,))))
    refs[-1][...] = total.astype(refs[-1].dtype)


def gather_add(dest, pieces, terms, returned, dtype):
    return pl.pallas_call(
        functools.partial(gather_add_kernel, pieces, len(terms)),
        out_shape=jax.ShapeDtypeStruct(terms[0].shape, dtype),
        in_specs=[IN_VMEM] * (1 + len(terms) + len(returned)),
        out_specs=IN_VMEM,
        compiler_params=params(),
        cost_estimate=CHEAP,
        name="gather_add",
    )(dest, *terms, *returned)


def along(x, pairs):
    return lax.ppermute(x, "own", pairs)


def shifted(x, shift):
    size = lax.axis_size("own")
    return along(x, [(i, (i + shift) % size) for i in range(size)])


def opposite(before, after):
    return along(before, [(0, 1), (2, 3)]), along(after, [(1, 0), (3, 2)])


def partner(x, bit):
    return lax.ppermute(x, "tp", [(i, i ^ bit) for i in range(lax.axis_size("tp"))])


def two_terms(x):
    bit = 1
    while 2 * bit < lax.axis_size("tp"):
        x = x + partner(x, bit)
        bit *= 2
    return x, partner(x, bit)


def base_terms(me, tokens, value, parts):
    kept, away = base_blocks(me, tokens, value, parts)
    bit = 1
    while 2 * bit < parts:
        total = kept + partner(away, bit)
        blocks = jnp.split(total, parts // (2 * bit), axis=1)
        bit *= 2
        kept, away = (jnp.concatenate(blocks[k::2], axis=1) if len(blocks) > 2 else blocks[k] for k in range(2))
    return kept, partner(away, bit)


def direct(tokens, token_adapter_index, adapter_storage_row, value_matrix, down_stored, up_stored):
    owners, parts = lax.axis_size("own"), lax.axis_size("tp")
    count = tokens.shape[0]
    holder, _, rank = down_stored.shape
    cap = CAP * (2 * count // CAP // owners)
    first = cap * 5 // 8 // 16 * 16
    late = cap - first
    me = lax.axis_index("own").astype(jnp.int32).reshape(1)
    me_part = lax.axis_index("tp").astype(jnp.int32).reshape(1)
    index_row = token_adapter_index.reshape(1, count)
    storage_row = adapter_storage_row.reshape(1, -1)
    down = jnp.swapaxes(down_stored, 1, 2).reshape(holder * rank, -1)
    up = up_stored.reshape(holder * rank, -1)
    shifts = list(range(1, owners))
    late_start = (owners - 1) * first

    mains = {s: ((s - 1) * first, first) for s in shifts}
    size = first + late
    *packed, dest, home_ids, more = route_pack(me, index_row, storage_row, tokens, owners, holder, first, late)
    packed, me_part, home_ids = lax.optimization_barrier((packed, me_part, home_ids))
    below, above = shifted(packed[0], 1), shifted(packed[2], 3)
    base = base_terms(me_part, tokens, value_matrix, parts)
    lows = two_terms(low_rank_home(home_ids, down, tokens, holder))
    (stays,) = up_project(home_ids, up, *lows, holder)
    total = gather_add(dest, [], [*base, ADAPTER_SCALE * stays], [], F32)
    rest, above = lax.optimization_barrier((packed[1], above))
    across = shifted(rest, 2)
    below, above, total = lax.optimization_barrier((below, above, total))
    far = opposite(below[first:], above[first:])
    blocks = [(size, [(j, 0)], [(j, size)], s - 1, 0) for j, s in enumerate((1, 3))]
    lows, ids, near_more = low_rank(me, down, blocks, [below, above], holder)
    near = up_project(ids, up, *two_terms(lows), holder)
    back = [shifted(x, -s) for s, x in zip((1, 3), near)]
    pieces = [(*mains[1], [(0, 0)]), (*mains[3], [(1, 0)]), (late_start, late, [(0, first), (1, first)])]
    total = gather_add(dest, pieces, [total], back, F32)

    def second(total):
        x = repack(index_row, storage_row, dest, tokens, late_start + late, late)
        below, above = shifted(x, 1), shifted(x, 3)
        x = [below, *opposite(below, above), above]
        sources = [[0], [1, 2], [3]]
        blocks = [(late, [(j, 0) for j in js], [(j, late) for j in js], 0, 0) for js in sources]
        lows, ids, _ = low_rank(me, down, blocks, x, holder)
        done = up_project(ids, up, *two_terms(lows), holder)
        back = [shifted(x, -s) for s, x in zip(shifts, done)]
        return gather_add(dest, [(late_start + late, late, [(j, 0) for j in range(3)])], [total], back, F32)

    across, far, near = lax.optimization_barrier((across, far, near))
    tags = [(j, late) for j in (1, 2)]
    joined = [(first, [(0, 0)], tags, 1, 0), (late, [(1, 0), (2, 0)], tags, 1, first)]
    lows, ids, far_more = low_rank(me, down, joined, [across, *far], holder, joined=True)
    (done,) = up_project(ids, up, *two_terms(lows), holder)
    more = jnp.maximum(more[0], jnp.maximum(near_more[0], far_more[0]))
    total = lax.cond(more > 0, second, lambda total: total, total)
    back = shifted(done, -2)
    pieces = [(*mains[2], [(0, 0)]), (late_start, late, [(0, first)])]
    return gather_add(dest, pieces, [total], [back], BF16)


def by_all_to_all(tokens, token_adapter_index, adapter_storage_row, value_matrix, down_stored, up_stored):
    owners = lax.axis_size("own")
    tok_dev, features = tokens.shape
    holder, _, rank = down_stored.shape
    cap = CAP * (2 * tok_dev // CAP // owners)
    slots = owners * cap
    catalog = jnp.arange(adapter_storage_row.shape[0], dtype=jnp.int32)
    storage = jnp.sum(
        jnp.where(token_adapter_index[:, None] == catalog[None, :], adapter_storage_row[None, :], 0), axis=1
    )
    home_owner = storage // holder
    hits = (home_owner[:, None] == jnp.arange(owners, dtype=jnp.int32)[None, :]).astype(jnp.int32)
    before = jnp.cumsum(hits, axis=0) - hits
    dest = home_owner * cap + jnp.sum(before * hits, axis=1)
    outgoing = jnp.zeros((slots, features), tokens.dtype).at[dest].set(tokens)
    which = jnp.full((slots,), holder, jnp.int32).at[dest].set(storage % holder)
    base = jnp.dot(tokens, value_matrix, preferred_element_type=F32)
    rows_in = lax.all_to_all(
        outgoing.reshape(owners, cap, features), "own", split_axis=0, concat_axis=0, tiled=True
    ).reshape(slots, features)
    which = lax.all_to_all(which.reshape(owners, cap), "own", split_axis=0, concat_axis=0, tiled=True)
    selector = (which.reshape(slots)[:, None] == jnp.arange(holder)[None, :]).astype(F32)
    every = jnp.einsum("nf,afr->nar", rows_in, down_stored, preferred_element_type=F32)
    low = lax.psum(jnp.sum(every * selector[:, :, None], axis=1), "tp")
    spread = (selector[:, :, None] * low[:, None, :]).reshape(slots, holder * rank)
    stacked = up_stored.reshape(holder * rank, -1).astype(F32)
    term = jnp.dot(spread, stacked, precision=lax.Precision.HIGHEST).reshape(owners, cap, -1)
    term = lax.all_to_all(term, "own", split_axis=0, concat_axis=0, tiled=True).reshape(slots, -1)[dest]
    mixed = lax.psum_scatter(base, "tp", scatter_dimension=1, tiled=True) + ADAPTER_SCALE * term
    return mixed.astype(BF16)


def solution(mesh):
    owners, parts = mesh.shape["own"], mesh.shape["tp"]
    on_a_line = owners == LINE and parts > 1 and parts & (parts - 1) == 0
    body = direct if on_a_line else by_all_to_all
    return jax.shard_map(
        body,
        mesh=mesh,
        in_specs=(
            P(("rep", "own"), "tp"),
            P(("rep", "own")),
            P("rep"),
            P("tp", None),
            P(("rep", "own"), "tp", None),
            P(("rep", "own"), None, "tp"),
        ),
        out_specs=P(("rep", "own"), "tp"),
        check_vma=False,
    )
```

```python
import functools

import jax
import jax.numpy as jnp
from jax import lax
from jax.experimental import pallas as pl
from jax.experimental.pallas import tpu as pltpu
from jax.sharding import PartitionSpec as P

CAP = 4
ADAPTER_SCALE = 0.5
TAGS = 16
CODE_ROWS = 16
LINE = 4
BF16 = jnp.bfloat16
F32 = jnp.float32
VMEM_LIMIT = 16 * 2**20
CHEAP = pl.CostEstimate(flops=1, bytes_accessed=1, transcendentals=0)


def params(**kw):
    return pltpu.CompilerParams(vmem_limit_bytes=VMEM_LIMIT, **kw)


def iota(shape, dim):
    return lax.broadcasted_iota(jnp.int32, shape, dim)


def dot(a, b, dims=((1,), (0,))):
    return lax.dot_general(a, b, (dims, ((), ())), preferred_element_type=F32)


def split_bf16(x):
    high = x.astype(BF16)
    return high, (x - high.astype(F32)).astype(BF16)


def one_hot(mask):
    return mask.astype(F32).astype(BF16)


IN_VMEM = pl.BlockSpec(memory_space=pltpu.VMEM)
IN_SMEM = pl.BlockSpec(memory_space=pltpu.SMEM)


def storage_of(index_row, storage_row):
    adapters = storage_row.shape[1]
    square = (adapters, adapters)
    diagonal = jnp.where(iota(square, 0) == iota(square, 1), storage_row.astype(F32), 0.0)
    column = jnp.sum(diagonal, axis=1, keepdims=True)
    shape = (adapters, index_row.shape[1])
    picked = jnp.where(iota(shape, 0) == index_row, column, 0.0)
    return jnp.sum(picked, axis=0, keepdims=True).astype(jnp.int32)


def owner_of(storage, holder, owners):
    owner = jnp.zeros_like(storage)
    for k in range(1, owners):
        owner = owner + (storage >= k * holder).astype(jnp.int32)
    return owner


def earlier(tokens):
    return one_hot(iota((tokens, tokens), 0) < iota((tokens, tokens), 1))


def routes(index_row, storage_row, holder, owners, group, first):
    tokens = index_row.shape[1]
    storage = storage_of(index_row, storage_row)
    owner = owner_of(storage, holder, owners)
    strict = earlier(tokens)
    rows = -(-owners // 8) * 8
    hits = iota((rows, tokens), 0) == owner
    rank = jnp.sum(jnp.where(hits, dot(one_hot(hits), strict), 0.0), axis=0, keepdims=True)
    late = jnp.where((owner != group) & (rank >= first), 1.0, 0.0)
    place = dot(jnp.broadcast_to(late, (8, tokens)).astype(BF16), strict)[0:1, :]
    late_place = jnp.where(late > 0, place, -1.0).astype(jnp.int32)
    return owner, storage, rank.astype(jnp.int32), late_place


def known_adapters(storage, picks, flag):
    tokens = storage.shape[1]
    known = jnp.broadcast_to((storage + 1).astype(F32), (8, tokens)).astype(BF16)
    width = picks[0].shape[0]
    which = iota((TAGS, width), 0)
    tags = jnp.where(which == TAGS - 1, flag, 0.0)
    for k, pick in enumerate(picks):
        row = dot(known, pick, ((1,), (1,)))
        tags = jnp.where(which == k, jnp.concatenate([row] * (TAGS // 8), axis=0), tags)
    return tags.astype(BF16)


def route_pack_kernel(owners, holder, first, late, me_ref, index_hbm, storage_hbm, tokens_hbm, *refs):
    outs, (dest_ref, home_ids_ref, more_ref, picks, index, storage, tokens, sems) = refs[:3], refs[3:]
    tiles, _, tile = tokens.shape
    small = [pltpu.make_async_copy(index_hbm, index, sems.at[tiles])]
    small += [pltpu.make_async_copy(storage_hbm, storage, sems.at[tiles + 1])]
    large = [
        pltpu.make_async_copy(tokens_hbm.at[:, pl.ds(i * tile, tile)], tokens.at[i], sems.at[i])
        for i in range(tiles)
    ]
    for copy in small + large:
        copy.start()
    for copy in small:
        copy.wait()
    me = me_ref[0]
    owner, row, rank, place = routes(index[...], storage[...], holder, owners, me, first)
    home_ids_ref[...] = jnp.where(owner == me, row - me * holder, -1)
    away = owner - me
    away = jnp.where(away < 0, away + owners, away)
    dest = jnp.where(place >= 0, (owners - 1) * first + place, (away - 1) * first + rank)
    dest_ref[...] = jnp.where(away == 0, -1, dest)
    more = (jnp.max(place) >= late).astype(jnp.int32)
    more_ref[0] = more
    for s in range(1, owners):
        slot = jnp.where(place >= 0, first + place, jnp.where(away == s, rank, -1))
        picks[s - 1] = one_hot(iota(picks.shape[1:], 0) == slot)
    tags = known_adapters(row, [picks[s - 1] for s in range(1, owners)], more.astype(F32))
    size = first + late
    for out in (outs[0], outs[2]):
        out[size:, :] = jnp.zeros((TAGS, out.shape[1]), BF16)
        out[size:, 0:size] = tags
    for i, copy in enumerate(large):
        copy.wait()
        at = slice(i * tile, (i + 1) * tile)
        for s, rows in ((1, size), (3, first), (2, first)):
            if s == 3:
                outs[2][0:first, at] = dot(picks[2, 0:first, :], tokens[i]).astype(BF16)
                outs[2][first:size, at] = outs[0][first:size, at]
            else:
                outs[s - 1][0:rows, at] = dot(picks[s - 1, 0:rows, :], tokens[i]).astype(BF16)


def route_pack(me, index_row, storage_row, tokens, owners, holder, first, late):
    count, features = tokens.shape
    tiles = 4 if features % 512 == 0 else 1
    in_hbm = pl.BlockSpec(memory_space=pltpu.HBM)
    long = first + late + TAGS
    return pl.pallas_call(
        functools.partial(route_pack_kernel, owners, holder, first, late),
        out_shape=[jax.ShapeDtypeStruct((rows, features), BF16) for rows in (long, first, long)]
        + [jax.ShapeDtypeStruct((1, count), jnp.int32)] * 2
        + [jax.ShapeDtypeStruct((1,), jnp.int32)],
        in_specs=[IN_SMEM, in_hbm, in_hbm, in_hbm],
        out_specs=[IN_VMEM] * 5 + [IN_SMEM],
        scratch_shapes=[
            pltpu.VMEM((owners - 1, first + late, count), BF16),
            pltpu.VMEM(index_row.shape, jnp.int32),
            pltpu.VMEM(storage_row.shape, jnp.int32),
            pltpu.VMEM((tiles, count, features // tiles), BF16),
            pltpu.SemaphoreType.DMA((tiles + 2,)),
        ],
        compiler_params=params(),
        cost_estimate=CHEAP,
        name="route_pack",
    )(me, index_row, storage_row, tokens)


def repack_kernel(start, index_ref, storage_ref, dest_ref, tokens_ref, out):
    rows = out.shape[0] - TAGS
    pick = one_hot(iota((rows, dest_ref.shape[1]), 0) + start == dest_ref[...])
    out[0:rows, :] = dot(pick, tokens_ref[...]).astype(BF16)
    out[rows:, :] = jnp.zeros((TAGS, out.shape[1]), BF16)
    out[rows:, 0:rows] = known_adapters(storage_of(index_ref[...], storage_ref[...]), [pick], 0.0)


def repack(index_row, storage_row, dest, tokens, start, rows):
    return pl.pallas_call(
        functools.partial(repack_kernel, start),
        out_shape=jax.ShapeDtypeStruct((rows + TAGS, tokens.shape[1]), BF16),
        in_specs=[IN_VMEM] * 4,
        out_specs=IN_VMEM,
        compiler_params=params(),
        name="repack",
    )(index_row, storage_row, dest, tokens)


def low_rank_kernel(blocks, joined, holder, rank, me_ref, down_ref, *refs):
    out, ids_out, flag = refs[-3:]
    lead = me_ref[0] * holder + 1
    flags = jnp.zeros((1, 1), F32)
    for k, (rows, sources, tagged, row, tag_start) in enumerate(blocks):
        rows_in = functools.reduce(jnp.add, [refs[j][at : at + rows, :] for j, at in sources])
        every = dot(down_ref[...], rows_in, ((1,), (1,)))
        tags = functools.reduce(jnp.add, [refs[j][at : at + TAGS, :].astype(F32) for j, at in tagged])
        flags = jnp.maximum(flags, tags[TAGS - 1 : TAGS, 0:1])
        ids = tags[row : row + 1, tag_start : tag_start + rows].astype(jnp.int32) - lead
        total = jnp.zeros((rank, rows), F32)
        for a in range(holder):
            total = total + jnp.where(ids == a, every[a * rank : (a + 1) * rank, :], 0.0)
        at = slice(tag_start, tag_start + rows)
        if joined:
            out[:, at] = total
            ids_out[:, at] = ids
        else:
            out[k * rank : (k + 1) * rank, :] = total
            ids_out[k : k + 1, :] = ids
    flag[0] = jnp.max(flags).astype(jnp.int32)


def low_rank(me, down, blocks, messages, holder, joined=False):
    rank = down.shape[0] // holder
    rows = sum(block[0] for block in blocks) if joined else blocks[0][0]
    number = 1 if joined else len(blocks)
    return pl.pallas_call(
        functools.partial(low_rank_kernel, blocks, joined, holder, rank),
        out_shape=[
            jax.ShapeDtypeStruct((number * rank, rows), F32),
            jax.ShapeDtypeStruct((number, rows), jnp.int32),
            jax.ShapeDtypeStruct((1,), jnp.int32),
        ],
        in_specs=[IN_SMEM] + [IN_VMEM] * (1 + len(messages)),
        out_specs=[IN_VMEM, IN_VMEM, IN_SMEM],
        compiler_params=params(),
        cost_estimate=CHEAP,
        name="low_rank",
    )(me, down, *messages)


def low_rank_home_kernel(holder, rank, ids_ref, down_ref, tokens_ref, out):
    every = dot(down_ref[...], tokens_ref[...], ((1,), (1,)))
    ids = ids_ref[...]
    total = jnp.zeros(out.shape, F32)
    for a in range(holder):
        total = total + jnp.where(ids == a, every[a * rank : (a + 1) * rank, :], 0.0)
    out[...] = total


def low_rank_home(ids, down, tokens, holder):
    rank = down.shape[0] // holder
    return pl.pallas_call(
        functools.partial(low_rank_home_kernel, holder, rank),
        out_shape=jax.ShapeDtypeStruct((rank, tokens.shape[0]), F32),
        in_specs=[IN_VMEM] * 3,
        out_specs=IN_VMEM,
        compiler_params=params(),
        cost_estimate=CHEAP,
        name="low_rank_home",
    )(ids, down, tokens)


def up_kernel(rows, holder, rank, ids_ref, up_ref, a_ref, b_ref, *outs):
    up = up_ref[...]
    for k, out in enumerate(outs):
        own = slice(k * rank, (k + 1) * rank)
        low = a_ref[own, :] + b_ref[own, :]
        ids = ids_ref[k : k + 1, :]
        spread = jnp.concatenate([jnp.where(ids == a, low, 0.0) for a in range(holder)], axis=0)
        high, rest = split_bf16(spread)
        out[...] = dot(high, up, ((0,), (0,))) + dot(rest, up, ((0,), (0,)))


def up_project(ids, up, a, b, holder):
    blocks, rows = ids.shape
    rank = up.shape[0] // holder
    return pl.pallas_call(
        functools.partial(up_kernel, rows, holder, rank),
        out_shape=[jax.ShapeDtypeStruct((rows, up.shape[1]), F32)] * blocks,
        in_specs=[IN_VMEM] * 4,
        out_specs=[IN_VMEM] * blocks,
        compiler_params=params(),
        cost_estimate=CHEAP,
        name="up_project",
    )(ids, up, a, b)


def up_coded_kernel(holder, rank, ids_ref, up_ref, a_ref, b_ref, *outs):
    up = up_ref[...]
    width = up.shape[1]
    for k, out in enumerate(outs):
        own = slice(k * rank, (k + 1) * rank)
        low = a_ref[own, :] + b_ref[own, :]
        ids = ids_ref[k : k + 1, :]
        spread = jnp.concatenate([jnp.where(ids == a, low, 0.0) for a in range(holder)], axis=0)
        high, rest = split_bf16(spread)
        term = ADAPTER_SCALE * (dot(up, high, ((0,), (0,))) + dot(up, rest, ((0,), (0,))))
        largest = jnp.maximum(jnp.max(jnp.abs(term), axis=0, keepdims=True), 1e-30)
        exponent = jnp.floor(jnp.log2(largest)) + 1.0
        code = jnp.clip(jnp.round(term * jnp.exp2(15.0 - exponent)), -32767.0, 32767.0)
        out[0:width, :] = code.astype(jnp.int32).astype(jnp.int16)
        exponents = jnp.broadcast_to(exponent, (out.shape[0] - width, out.shape[1]))
        out[width:, :] = exponents.astype(jnp.int32).astype(jnp.int16)


def up_coded(ids, up, a, b, holder):
    blocks, rows = ids.shape
    rank = up.shape[0] // holder
    return pl.pallas_call(
        functools.partial(up_coded_kernel, holder, rank),
        out_shape=[jax.ShapeDtypeStruct((up.shape[1] + CODE_ROWS, rows), jnp.int16)] * blocks,
        in_specs=[IN_VMEM] * 4,
        out_specs=[IN_VMEM] * blocks,
        compiler_params=params(),
        cost_estimate=CHEAP,
        name="up_coded",
    )(ids, up, a, b)


def base_kernel(parts, me_ref, tokens_ref, value_ref, kept_ref, away_ref, full):
    width = full.shape[1] // parts
    full[...] = dot(tokens_ref[...], value_ref[...])
    for q in range(parts):
        block = me_ref[0] ^ q
        at = pl.ds(q // 2 * width, width)
        (away_ref if q % 2 else kept_ref)[:, at] = full[:, pl.ds(pl.multiple_of(block * width, width), width)]


def base_blocks(me, tokens, value, parts):
    count, columns = tokens.shape[0], value.shape[1]
    return pl.pallas_call(
        functools.partial(base_kernel, parts),
        out_shape=[jax.ShapeDtypeStruct((count, columns // 2), F32)] * 2,
        in_specs=[IN_SMEM, IN_VMEM, IN_VMEM],
        out_specs=[IN_VMEM, IN_VMEM],
        scratch_shapes=[pltpu.VMEM((count, columns), F32)],
        compiler_params=params(),
        cost_estimate=CHEAP,
        name="base_blocks",
    )(me, tokens, value)


def gather_add_kernel(ranges, terms, dest_ref, *refs):
    total = refs[0][...]
    for k in range(1, terms):
        total = total + refs[k][...]
    dest = dest_ref[...]
    found = jnp.zeros((total.shape[1], total.shape[0]), F32)
    for (start, rows, late_start), ref in zip(ranges, refs[terms:]):
        width = total.shape[1]
        exponent = ref[width:, :].astype(jnp.int32).astype(F32)[0:1, :]
        values = ref[0:width, :].astype(jnp.int32).astype(F32) * jnp.exp2(exponent - 15.0)
        shape = (values.shape[1], dest.shape[1])
        row = iota(shape, 0)
        pick = one_hot(jnp.where(row < rows, row + start, row + (late_start - rows)) == dest)
        high, rest = split_bf16(values)
        found = found + (dot(high, pick) + dot(rest, pick))
    if ranges:
        total = total + found.T
    refs[-1][...] = total.astype(refs[-1].dtype)


def gather_add(dest, ranges, terms, returned, dtype):
    return pl.pallas_call(
        functools.partial(gather_add_kernel, ranges, len(terms)),
        out_shape=jax.ShapeDtypeStruct(terms[0].shape, dtype),
        in_specs=[IN_VMEM] * (1 + len(terms) + len(returned)),
        out_specs=IN_VMEM,
        compiler_params=params(),
        cost_estimate=CHEAP,
        name="gather_add",
    )(dest, *terms, *returned)


def along(x, pairs):
    return lax.ppermute(x, "own", pairs)


def shifted(x, shift):
    size = lax.axis_size("own")
    return along(x, [(i, (i + shift) % size) for i in range(size)])


def opposite(before, after):
    return along(before, [(0, 1), (2, 3)]), along(after, [(1, 0), (3, 2)])


def partner(x, bit):
    return lax.ppermute(x, "tp", [(i, i ^ bit) for i in range(lax.axis_size("tp"))])


def two_terms(x):
    bit = 1
    while 2 * bit < lax.axis_size("tp"):
        x = x + partner(x, bit)
        bit *= 2
    return x, partner(x, bit)


def base_terms(me, tokens, value, parts):
    kept, away = base_blocks(me, tokens, value, parts)
    bit = 1
    while 2 * bit < parts:
        total = kept + partner(away, bit)
        blocks = jnp.split(total, parts // (2 * bit), axis=1)
        bit *= 2
        kept, away = (jnp.concatenate(blocks[k::2], axis=1) if len(blocks) > 2 else blocks[k] for k in range(2))
    return kept, partner(away, bit)


def direct(tokens, token_adapter_index, adapter_storage_row, value_matrix, down_stored, up_stored):
    owners, parts = lax.axis_size("own"), lax.axis_size("tp")
    count = tokens.shape[0]
    holder, _, rank = down_stored.shape
    cap = CAP * (2 * count // CAP // owners)
    first = cap * 5 // 8 // 16 * 16
    late = cap - first
    me = lax.axis_index("own").astype(jnp.int32).reshape(1)
    me_part = lax.axis_index("tp").astype(jnp.int32).reshape(1)
    index_row = token_adapter_index.reshape(1, count)
    storage_row = adapter_storage_row.reshape(1, -1)
    down = jnp.swapaxes(down_stored, 1, 2).reshape(holder * rank, -1)
    up = up_stored.reshape(holder * rank, -1)
    shifts = list(range(1, owners))
    late_start = (owners - 1) * first

    mains = {s: ((s - 1) * first, first) for s in shifts}
    size = first + late
    *packed, dest, home_ids, more = route_pack(me, index_row, storage_row, tokens, owners, holder, first, late)
    packed, me_part, home_ids = lax.optimization_barrier((packed, me_part, home_ids))
    below, above = shifted(packed[0], 1), shifted(packed[2], 3)
    base = base_terms(me_part, tokens, value_matrix, parts)
    lows = two_terms(low_rank_home(home_ids, down, tokens, holder))
    (stays,) = up_project(home_ids, up, *lows, holder)
    total = gather_add(dest, [], [*base, ADAPTER_SCALE * stays], [], F32)
    rest, above = lax.optimization_barrier((packed[1], above))
    across = shifted(rest, 2)
    below, above, total = lax.optimization_barrier((below, above, total))
    far = opposite(below[first:], above[first:])
    blocks = [(size, [(j, 0)], [(j, size)], s - 1, 0) for j, s in enumerate((1, 3))]
    lows, ids, near_more = low_rank(me, down, blocks, [below, above], holder)
    near = up_coded(ids, up, *two_terms(lows), holder)
    back = [shifted(x, -s) for s, x in zip((1, 3), near)]
    total = gather_add(dest, [(*mains[s], late_start) for s in (1, 3)], [total], back, F32)

    def second(total):
        x = repack(index_row, storage_row, dest, tokens, late_start + late, late)
        below, above = shifted(x, 1), shifted(x, 3)
        x = [below, *opposite(below, above), above]
        sources = [[0], [1, 2], [3]]
        blocks = [(late, [(j, 0) for j in js], [(j, late) for j in js], 0, 0) for js in sources]
        lows, ids, _ = low_rank(me, down, blocks, x, holder)
        done = up_coded(ids, up, *two_terms(lows), holder)
        back = [shifted(x, -s) for s, x in zip(shifts, done)]
        return gather_add(dest, [(late_start + late, late, 0)] * len(back), [total], back, F32)

    across, far, near = lax.optimization_barrier((across, far, near))
    tags = [(j, late) for j in (1, 2)]
    joined = [(first, [(0, 0)], tags, 1, 0), (late, [(1, 0), (2, 0)], tags, 1, first)]
    lows, ids, far_more = low_rank(me, down, joined, [across, *far], holder, joined=True)
    (done,) = up_coded(ids, up, *two_terms(lows), holder)
    more = jnp.maximum(more[0], jnp.maximum(near_more[0], far_more[0]))
    total = lax.cond(more > 0, second, lambda total: total, total)
    back = shifted(done, -2)
    return gather_add(dest, [(*mains[2], late_start)], [total], [back], BF16)


def by_all_to_all(tokens, token_adapter_index, adapter_storage_row, value_matrix, down_stored, up_stored):
    owners = lax.axis_size("own")
    tok_dev, features = tokens.shape
    holder, _, rank = down_stored.shape
    cap = CAP * (2 * tok_dev // CAP // owners)
    slots = owners * cap
    catalog = jnp.arange(adapter_storage_row.shape[0], dtype=jnp.int32)
    storage = jnp.sum(
        jnp.where(token_adapter_index[:, None] == catalog[None, :], adapter_storage_row[None, :], 0), axis=1
    )
    home_owner = storage // holder
    hits = (home_owner[:, None] == jnp.arange(owners, dtype=jnp.int32)[None, :]).astype(jnp.int32)
    before = jnp.cumsum(hits, axis=0) - hits
    dest = home_owner * cap + jnp.sum(before * hits, axis=1)
    outgoing = jnp.zeros((slots, features), tokens.dtype).at[dest].set(tokens)
    which = jnp.full((slots,), holder, jnp.int32).at[dest].set(storage % holder)
    base = jnp.dot(tokens, value_matrix, preferred_element_type=F32)
    rows_in = lax.all_to_all(
        outgoing.reshape(owners, cap, features), "own", split_axis=0, concat_axis=0, tiled=True
    ).reshape(slots, features)
    which = lax.all_to_all(which.reshape(owners, cap), "own", split_axis=0, concat_axis=0, tiled=True)
    selector = (which.reshape(slots)[:, None] == jnp.arange(holder)[None, :]).astype(F32)
    every = jnp.einsum("nf,afr->nar", rows_in, down_stored, preferred_element_type=F32)
    low = lax.psum(jnp.sum(every * selector[:, :, None], axis=1), "tp")
    spread = (selector[:, :, None] * low[:, None, :]).reshape(slots, holder * rank)
    stacked = up_stored.reshape(holder * rank, -1).astype(F32)
    term = jnp.dot(spread, stacked, precision=lax.Precision.HIGHEST).reshape(owners, cap, -1)
    term = lax.all_to_all(term, "own", split_axis=0, concat_axis=0, tiled=True).reshape(slots, -1)[dest]
    mixed = lax.psum_scatter(base, "tp", scatter_dimension=1, tiled=True) + ADAPTER_SCALE * term
    return mixed.astype(BF16)


def solution(mesh):
    owners, parts = mesh.shape["own"], mesh.shape["tp"]
    on_a_line = owners == LINE and parts > 1 and parts & (parts - 1) == 0
    body = direct if on_a_line else by_all_to_all
    return jax.shard_map(
        body,
        mesh=mesh,
        in_specs=(
            P(("rep", "own"), "tp"),
            P(("rep", "own")),
            P("rep"),
            P("tp", None),
            P(("rep", "own"), "tp", None),
            P(("rep", "own"), None, "tp"),
        ),
        out_specs=P(("rep", "own"), "tp"),
        check_vma=False,
    )
```

```python
import functools

import jax
import jax.numpy as jnp
from jax import lax
from jax.experimental import pallas as pl
from jax.experimental.pallas import tpu as pltpu
from jax.sharding import PartitionSpec as P

CAP = 4
ADAPTER_SCALE = 0.5
CODE_ROWS = 16
LINE = 4
BF16 = jnp.bfloat16
F32 = jnp.float32
VMEM_LIMIT = 16 * 2**20
CHEAP = pl.CostEstimate(flops=1, bytes_accessed=1, transcendentals=0)


def params(**kw):
    return pltpu.CompilerParams(vmem_limit_bytes=VMEM_LIMIT, **kw)


def iota(shape, dim):
    return lax.broadcasted_iota(jnp.int32, shape, dim)


def dot(a, b, dims=((1,), (0,))):
    return lax.dot_general(a, b, (dims, ((), ())), preferred_element_type=F32)


def split_bf16(x):
    high = x.astype(BF16)
    return high, (x - high.astype(F32)).astype(BF16)


def one_hot(mask):
    return mask.astype(F32).astype(BF16)


IN_VMEM = pl.BlockSpec(memory_space=pltpu.VMEM)
IN_SMEM = pl.BlockSpec(memory_space=pltpu.SMEM)


def storage_of(index_row, storage_row):
    adapters = storage_row.shape[1]
    square = (adapters, adapters)
    diagonal = jnp.where(iota(square, 0) == iota(square, 1), storage_row.astype(F32), 0.0)
    column = jnp.sum(diagonal, axis=1, keepdims=True)
    shape = (adapters, index_row.shape[1])
    picked = jnp.where(iota(shape, 0) == index_row, column, 0.0)
    return jnp.sum(picked, axis=0, keepdims=True).astype(jnp.int32)


def owner_of(storage, holder, owners):
    owner = jnp.zeros_like(storage)
    for k in range(1, owners):
        owner = owner + (storage >= k * holder).astype(jnp.int32)
    return owner


def earlier(tokens):
    return one_hot(iota((tokens, tokens), 0) < iota((tokens, tokens), 1))


def routes(index_row, storage_row, holder, owners, group, first):
    tokens = index_row.shape[1]
    storage = storage_of(index_row, storage_row)
    owner = owner_of(storage, holder, owners)
    strict = earlier(tokens)
    rows = -(-owners // 8) * 8
    hits = iota((rows, tokens), 0) == owner
    rank = jnp.sum(jnp.where(hits, dot(one_hot(hits), strict), 0.0), axis=0, keepdims=True)
    late = jnp.where((owner != group) & (rank >= first), 1.0, 0.0)
    place = dot(jnp.broadcast_to(late, (8, tokens)).astype(BF16), strict)[0:1, :]
    late_place = jnp.where(late > 0, place, -1.0).astype(jnp.int32)
    return owner, storage, rank.astype(jnp.int32), late_place


def lanes(count):
    return -(-count // 128) * 128


def known_adapters(storage, picks, flag, features):
    tokens = storage.shape[1]
    known = jnp.broadcast_to((storage + 1).astype(F32), (8, tokens)).astype(BF16)
    sections = []
    for pick in picks:
        size = pick.shape[0]
        sections.append(dot(known, pick, ((1,), (1,))))
        if size % 128:
            sections.append(jnp.zeros((8, lanes(size) - size), F32))
    used = sum(x.shape[1] for x in sections)
    sections += [jnp.full((8, 128), flag, F32), jnp.zeros((8, features - used - 128), F32)]
    return jnp.concatenate(sections, axis=1)[0:1, :]


def last_row(rows, row):
    return rows + jnp.where(iota(rows.shape, 0) == rows.shape[0] - 1, row, 0.0)


def route_pack_kernel(owners, holder, first, late, me_ref, index_hbm, storage_hbm, tokens_hbm, *refs):
    out, dest_ref, home_ids_ref, more_ref, picks, tags, index, storage, tokens, sems = refs
    tiles, _, tile = tokens.shape
    small = [pltpu.make_async_copy(index_hbm, index, sems.at[tiles])]
    small += [pltpu.make_async_copy(storage_hbm, storage, sems.at[tiles + 1])]
    large = [
        pltpu.make_async_copy(tokens_hbm.at[:, pl.ds(i * tile, tile)], tokens.at[i], sems.at[i])
        for i in range(tiles)
    ]
    for copy in small + large:
        copy.start()
    for copy in small:
        copy.wait()
    me = me_ref[0]
    owner, row, rank, place = routes(index[...], storage[...], holder, owners, me, first)
    home_ids_ref[...] = jnp.where(owner == me, row - me * holder, -1)
    away = owner - me
    away = jnp.where(away < 0, away + owners, away)
    dest = jnp.where(place >= 0, (owners - 1) * first + place, (away - 1) * first + rank)
    dest_ref[...] = jnp.where(away == 0, -1, dest)
    more = (jnp.max(place) >= late).astype(jnp.int32)
    more_ref[0] = more
    for s in range(1, owners):
        slot = jnp.where(place >= 0, jnp.where(place < late, first + place, -1), jnp.where(away == s, rank, -1))
        picks[s - 1] = one_hot(iota(picks.shape[1:], 0) == slot)
    features = out.shape[1]
    tags[...] = known_adapters(row, [picks[s - 1] for s in range(1, owners)], more.astype(F32), features)
    for i, copy in enumerate(large):
        copy.wait()
        at = slice(i * tile, (i + 1) * tile)
        out[:, at] = last_row(dot(picks[owners - 2], tokens[i]), tags[:, at]).astype(BF16)


def route_pack(me, index_row, storage_row, tokens, owners, holder, first, late):
    count, features = tokens.shape
    tiles = 4 if features % 512 == 0 else 1
    in_hbm = pl.BlockSpec(memory_space=pltpu.HBM)
    long = first + late + 1
    return pl.pallas_call(
        functools.partial(route_pack_kernel, owners, holder, first, late),
        out_shape=[jax.ShapeDtypeStruct((long, features), BF16)]
        + [jax.ShapeDtypeStruct((1, count), jnp.int32)] * 2
        + [jax.ShapeDtypeStruct((1,), jnp.int32)],
        in_specs=[IN_SMEM, in_hbm, in_hbm, in_hbm],
        out_specs=[IN_VMEM] * 3 + [IN_SMEM],
        scratch_shapes=[
            pltpu.VMEM((owners - 1, long, count), BF16),
            pltpu.VMEM((1, features), F32),
            pltpu.VMEM(index_row.shape, jnp.int32),
            pltpu.VMEM(storage_row.shape, jnp.int32),
            pltpu.VMEM((tiles, count, features // tiles), BF16),
            pltpu.SemaphoreType.DMA((tiles + 2,)),
        ],
        compiler_params=params(),
        cost_estimate=CHEAP,
        name="route_pack",
    )(me, index_row, storage_row, tokens)


def pack_more_kernel(first, dest_ref, tokens_ref, third_ref, one_out, two_out):
    dest = dest_ref[...]
    for s, out in ((1, one_out), (2, two_out)):
        pick = one_hot(iota((first, dest.shape[1]), 0) + (s - 1) * first == dest)
        out[0:first, :] = dot(pick, tokens_ref[...]).astype(BF16)
    one_out[first:, :] = third_ref[first:, :]


def pack_more(dest, tokens, third, first):
    return pl.pallas_call(
        functools.partial(pack_more_kernel, first),
        out_shape=[jax.ShapeDtypeStruct(third.shape, BF16), jax.ShapeDtypeStruct((first, tokens.shape[1]), BF16)],
        in_specs=[IN_VMEM] * 3,
        out_specs=[IN_VMEM] * 2,
        compiler_params=params(),
        cost_estimate=CHEAP,
        name="pack_more",
    )(dest, tokens, third)


def repack_kernel(start, index_ref, storage_ref, dest_ref, tokens_ref, out):
    rows = out.shape[0] - 1
    row = iota((rows + 1, dest_ref.shape[1]), 0)
    pick = one_hot((row < rows) & (row + start == dest_ref[...]))
    tags = known_adapters(storage_of(index_ref[...], storage_ref[...]), [pick], 0.0, out.shape[1])
    out[...] = last_row(dot(pick, tokens_ref[...]), tags).astype(BF16)


def repack(index_row, storage_row, dest, tokens, start, rows):
    return pl.pallas_call(
        functools.partial(repack_kernel, start),
        out_shape=jax.ShapeDtypeStruct((rows + 1, tokens.shape[1]), BF16),
        in_specs=[IN_VMEM] * 4,
        out_specs=IN_VMEM,
        compiler_params=params(),
        name="repack",
    )(index_row, storage_row, dest, tokens)


def low_rank_kernel(blocks, joined, holder, rank, me_ref, down_ref, *refs):
    out, ids_out, flag = refs[-3:]
    lead = me_ref[0] * holder + 1
    flags = jnp.zeros((1, 1), F32)
    for k, (rows, sources, tagged, section, flag_at, column) in enumerate(blocks):
        rows_in = functools.reduce(jnp.add, [refs[j][at : at + rows, :] for j, at in sources])
        every = dot(down_ref[...], rows_in, ((1,), (1,)))
        tags = [refs[j][refs[j].shape[0] - 16 :, 0 : flag_at + 128].astype(F32)[15:16, :] for j in tagged]
        tags = functools.reduce(jnp.add, tags)
        flags = jnp.maximum(flags, tags[:, flag_at : flag_at + 1])
        ids = tags[:, section + column : section + column + rows].astype(jnp.int32) - lead
        total = jnp.zeros((rank, rows), F32)
        for a in range(holder):
            total = total + jnp.where(ids == a, every[a * rank : (a + 1) * rank, :], 0.0)
        at = slice(column, column + rows)
        if joined:
            out[:, at] = total
            ids_out[:, at] = ids
        else:
            out[k * rank : (k + 1) * rank, :] = total
            ids_out[k : k + 1, :] = ids
    flag[0] = jnp.max(flags).astype(jnp.int32)


def low_rank(me, down, blocks, messages, holder, joined=False):
    rank = down.shape[0] // holder
    rows = sum(block[0] for block in blocks) if joined else blocks[0][0]
    number = 1 if joined else len(blocks)
    return pl.pallas_call(
        functools.partial(low_rank_kernel, blocks, joined, holder, rank),
        out_shape=[
            jax.ShapeDtypeStruct((number * rank, rows), F32),
            jax.ShapeDtypeStruct((number, rows), jnp.int32),
            jax.ShapeDtypeStruct((1,), jnp.int32),
        ],
        in_specs=[IN_SMEM] + [IN_VMEM] * (1 + len(messages)),
        out_specs=[IN_VMEM, IN_VMEM, IN_SMEM],
        compiler_params=params(),
        cost_estimate=CHEAP,
        name="low_rank",
    )(me, down, *messages)


def low_rank_home_kernel(holder, rank, ids_ref, down_ref, tokens_ref, out):
    every = dot(down_ref[...], tokens_ref[...], ((1,), (1,)))
    ids = ids_ref[...]
    total = jnp.zeros(out.shape, F32)
    for a in range(holder):
        total = total + jnp.where(ids == a, every[a * rank : (a + 1) * rank, :], 0.0)
    out[...] = total


def low_rank_home(ids, down, tokens, holder):
    rank = down.shape[0] // holder
    return pl.pallas_call(
        functools.partial(low_rank_home_kernel, holder, rank),
        out_shape=jax.ShapeDtypeStruct((rank, tokens.shape[0]), F32),
        in_specs=[IN_VMEM] * 3,
        out_specs=IN_VMEM,
        compiler_params=params(),
        cost_estimate=CHEAP,
        name="low_rank_home",
    )(ids, down, tokens)


def up_kernel(rows, holder, rank, ids_ref, up_ref, a_ref, b_ref, *outs):
    up = up_ref[...]
    for k, out in enumerate(outs):
        own = slice(k * rank, (k + 1) * rank)
        low = a_ref[own, :] + b_ref[own, :]
        ids = ids_ref[k : k + 1, :]
        spread = jnp.concatenate([jnp.where(ids == a, low, 0.0) for a in range(holder)], axis=0)
        high, rest = split_bf16(spread)
        out[...] = dot(high, up, ((0,), (0,))) + dot(rest, up, ((0,), (0,)))


def up_project(ids, up, a, b, holder):
    blocks, rows = ids.shape
    rank = up.shape[0] // holder
    return pl.pallas_call(
        functools.partial(up_kernel, rows, holder, rank),
        out_shape=[jax.ShapeDtypeStruct((rows, up.shape[1]), F32)] * blocks,
        in_specs=[IN_VMEM] * 4,
        out_specs=[IN_VMEM] * blocks,
        compiler_params=params(),
        cost_estimate=CHEAP,
        name="up_project",
    )(ids, up, a, b)


def up_coded_kernel(holder, rank, ids_ref, up_ref, a_ref, b_ref, *outs):
    up = up_ref[...]
    for k, out in enumerate(outs):
        own = slice(k * rank, (k + 1) * rank)
        low = a_ref[own, :] + b_ref[own, :]
        ids = ids_ref[k : k + 1, :]
        spread = jnp.concatenate([jnp.where(ids == a, low, 0.0) for a in range(holder)], axis=0)
        high, rest = split_bf16(spread)
        term = ADAPTER_SCALE * (dot(high, up, ((0,), (0,))) + dot(rest, up, ((0,), (0,))))
        largest = jnp.maximum(jnp.max(jnp.abs(term), axis=1, keepdims=True), 1e-30)
        exponent = jnp.floor(jnp.log2(largest)) + 1.0
        code = jnp.clip(jnp.round(term * jnp.exp2(15.0 - exponent)), -32767.0, 32767.0)
        rows = term.shape[0]
        out[0:rows, :] = code.astype(jnp.int32).astype(jnp.int16)
        square = (rows, lanes(rows))
        exponent = jnp.sum(jnp.where(iota(square, 0) == iota(square, 1), exponent, 0.0), axis=0, keepdims=True)
        tail = jnp.zeros((CODE_ROWS, 128), F32)
        for j in range(lanes(rows) // 128):
            tail = jnp.where(iota(tail.shape, 0) == j, exponent[:, j * 128 : (j + 1) * 128], tail)
        out[rows:, :] = tail.astype(jnp.int32).astype(jnp.int16)


def up_coded(ids, up, a, b, holder):
    blocks, rows = ids.shape
    rank = up.shape[0] // holder
    return pl.pallas_call(
        functools.partial(up_coded_kernel, holder, rank),
        out_shape=[jax.ShapeDtypeStruct((rows + CODE_ROWS, up.shape[1]), jnp.int16)] * blocks,
        in_specs=[IN_VMEM] * 4,
        out_specs=[IN_VMEM] * blocks,
        compiler_params=params(),
        cost_estimate=CHEAP,
        name="up_coded",
    )(ids, up, a, b)


def base_kernel(parts, me_ref, tokens_ref, value_ref, kept_ref, away_ref, full):
    width = full.shape[1] // parts
    full[...] = dot(tokens_ref[...], value_ref[...])
    for q in range(parts):
        block = me_ref[0] ^ q
        at = pl.ds(q // 2 * width, width)
        (away_ref if q % 2 else kept_ref)[:, at] = full[:, pl.ds(pl.multiple_of(block * width, width), width)]


def base_blocks(me, tokens, value, parts):
    count, columns = tokens.shape[0], value.shape[1]
    return pl.pallas_call(
        functools.partial(base_kernel, parts),
        out_shape=[jax.ShapeDtypeStruct((count, columns // 2), F32)] * 2,
        in_specs=[IN_SMEM, IN_VMEM, IN_VMEM],
        out_specs=[IN_VMEM, IN_VMEM],
        scratch_shapes=[pltpu.VMEM((count, columns), F32)],
        compiler_params=params(),
        cost_estimate=CHEAP,
        name="base_blocks",
    )(me, tokens, value)


def gather_add_kernel(ranges, terms, dest_ref, *refs):
    total = refs[0][...]
    for k in range(1, terms):
        total = total + refs[k][...]
    dest = dest_ref[...]
    for (start, rows, late_start), ref in zip(ranges, refs[terms:]):
        size = ref.shape[0] - CODE_ROWS
        tail = ref[size:, :].astype(jnp.int32).astype(F32)
        diagonal = iota((128, 128), 0) == iota((128, 128), 1)
        exponents = [
            jnp.sum(jnp.where(diagonal, tail[j : j + 1, :], 0.0), axis=1, keepdims=True)[0 : min(128, size - j * 128), :]
            for j in range(lanes(size) // 128)
        ]
        scale = jnp.exp2(jnp.concatenate(exponents, axis=0) - 15.0)
        values = ref[0:size, :].astype(jnp.int32).astype(F32) * scale
        row = iota((size, dest.shape[1]), 0)
        pick = one_hot(jnp.where(row < rows, row + start, row + (late_start - rows)) == dest)
        high, rest = split_bf16(values)
        total = total + (dot(pick, high, ((0,), (0,))) + dot(pick, rest, ((0,), (0,))))
    refs[-1][...] = total.astype(refs[-1].dtype)


def gather_add(dest, ranges, terms, returned, dtype):
    return pl.pallas_call(
        functools.partial(gather_add_kernel, ranges, len(terms)),
        out_shape=jax.ShapeDtypeStruct(terms[0].shape, dtype),
        in_specs=[IN_VMEM] * (1 + len(terms) + len(returned)),
        out_specs=IN_VMEM,
        compiler_params=params(),
        cost_estimate=CHEAP,
        name="gather_add",
    )(dest, *terms, *returned)


def along(x, pairs):
    return lax.ppermute(x, "own", pairs)


def shifted(x, shift):
    size = lax.axis_size("own")
    return along(x, [(i, (i + shift) % size) for i in range(size)])


def opposite(before, after):
    even = lax.axis_index("own") % 2 == 0
    return along(jnp.where(even, before, after), [(0, 1), (1, 0), (2, 3), (3, 2)])


def partner(x, bit):
    return lax.ppermute(x, "tp", [(i, i ^ bit) for i in range(lax.axis_size("tp"))])


def two_terms(x):
    bit = 1
    while 2 * bit < lax.axis_size("tp"):
        x = x + partner(x, bit)
        bit *= 2
    return x, partner(x, bit)


def base_terms(kept, away, parts):
    bit = 1
    while 2 * bit < parts:
        total = kept + partner(away, bit)
        blocks = jnp.split(total, parts // (2 * bit), axis=1)
        bit *= 2
        kept, away = (jnp.concatenate(blocks[k::2], axis=1) if len(blocks) > 2 else blocks[k] for k in range(2))
    return kept, partner(away, bit)


def direct(tokens, token_adapter_index, adapter_storage_row, value_matrix, down_stored, up_stored):
    owners, parts = lax.axis_size("own"), lax.axis_size("tp")
    count = tokens.shape[0]
    holder, _, rank = down_stored.shape
    cap = CAP * (2 * count // CAP // owners)
    first = cap * 9 // 16 // 16 * 16
    late = cap - first + 15
    me = lax.axis_index("own").astype(jnp.int32).reshape(1)
    me_part = lax.axis_index("tp").astype(jnp.int32).reshape(1)
    index_row = token_adapter_index.reshape(1, count)
    storage_row = adapter_storage_row.reshape(1, -1)
    down = jnp.swapaxes(down_stored, 1, 2).reshape(holder * rank, -1)
    up = up_stored.reshape(holder * rank, -1)
    shifts = list(range(1, owners))
    late_start = (owners - 1) * first

    mains = {s: ((s - 1) * first, first) for s in shifts}
    size = first + late + 1
    part = lanes(size)
    flag_at = 3 * part
    third, dest, home_ids, more = route_pack(me, index_row, storage_row, tokens, owners, holder, first, late)
    third, me_part, home_ids = lax.optimization_barrier((third, me_part, home_ids))
    above = shifted(third, 3)
    blocks = base_blocks(me_part, tokens, value_matrix, parts)
    blocks, dest = lax.optimization_barrier((blocks, dest))
    one, two = pack_more(dest, tokens, third, first)
    below = shifted(one, 1)
    base = base_terms(*blocks, parts)
    lows = two_terms(low_rank_home(home_ids, down, tokens, holder))
    (stays,) = up_project(home_ids, up, *lows, holder)
    total = gather_add(dest, [], [*base, ADAPTER_SCALE * stays], [], F32)
    rest, above, total = lax.optimization_barrier((two, above, total))
    across = shifted(rest, 2)

    def near_round(s, message):
        lows, ids, more = low_rank(me, down, [(size, [(0, 0)], [0], (s - 1) * part, flag_at, 0)], [message], holder)
        (done,) = up_coded(ids, up, *two_terms(lows), holder)
        return done, more

    above_done, above_more = near_round(3, above)
    above_back = shifted(above_done, -3)
    below, above_done = lax.optimization_barrier((below, above_done))
    far = opposite(below[first:], above[first:])
    below_done, below_more = near_round(1, below)
    near = [below_done, above_done]
    near_more = jnp.maximum(below_more, above_more)
    back = [shifted(below_done, -1), above_back]
    total = gather_add(dest, [(*mains[s], late_start) for s in (1, 3)], [total], back, F32)

    def second(total):
        x = repack(index_row, storage_row, dest, tokens, late_start + late, late)
        below, above = shifted(x, 1), shifted(x, 3)
        x = [below, opposite(below, above), above]
        sources = [[0], [1], [2]]
        blocks = [(late + 1, [(j, 0) for j in js], js, 0, lanes(late + 1), 0) for js in sources]
        lows, ids, _ = low_rank(me, down, blocks, x, holder)
        done = up_coded(ids, up, *two_terms(lows), holder)
        back = [shifted(x, -s) for s, x in zip(shifts, done)]
        return gather_add(dest, [(late_start + late, late + 1, 0)] * len(back), [total], back, F32)

    across, far, near = lax.optimization_barrier((across, far, near))
    joined = [
        (first, [(0, 0)], [1], part, flag_at, 0),
        (late + 1, [(1, 0)], [1], part, flag_at, first),
    ]
    lows, ids, far_more = low_rank(me, down, joined, [across, far], holder, joined=True)
    (done,) = up_coded(ids, up, *two_terms(lows), holder)
    more = jnp.maximum(more[0], jnp.maximum(near_more[0], far_more[0]))
    total = lax.cond(more > 0, second, lambda total: total, total)
    back = shifted(done, -2)
    return gather_add(dest, [(*mains[2], late_start)], [total], [back], BF16)


def by_all_to_all(tokens, token_adapter_index, adapter_storage_row, value_matrix, down_stored, up_stored):
    owners = lax.axis_size("own")
    tok_dev, features = tokens.shape
    holder, _, rank = down_stored.shape
    cap = CAP * (2 * tok_dev // CAP // owners)
    slots = owners * cap
    catalog = jnp.arange(adapter_storage_row.shape[0], dtype=jnp.int32)
    storage = jnp.sum(
        jnp.where(token_adapter_index[:, None] == catalog[None, :], adapter_storage_row[None, :], 0), axis=1
    )
    home_owner = storage // holder
    hits = (home_owner[:, None] == jnp.arange(owners, dtype=jnp.int32)[None, :]).astype(jnp.int32)
    before = jnp.cumsum(hits, axis=0) - hits
    dest = home_owner * cap + jnp.sum(before * hits, axis=1)
    outgoing = jnp.zeros((slots, features), tokens.dtype).at[dest].set(tokens)
    which = jnp.full((slots,), holder, jnp.int32).at[dest].set(storage % holder)
    base = jnp.dot(tokens, value_matrix, preferred_element_type=F32)
    rows_in = lax.all_to_all(
        outgoing.reshape(owners, cap, features), "own", split_axis=0, concat_axis=0, tiled=True
    ).reshape(slots, features)
    which = lax.all_to_all(which.reshape(owners, cap), "own", split_axis=0, concat_axis=0, tiled=True)
    selector = (which.reshape(slots)[:, None] == jnp.arange(holder)[None, :]).astype(F32)
    every = jnp.einsum("nf,afr->nar", rows_in, down_stored, preferred_element_type=F32)
    low = lax.psum(jnp.sum(every * selector[:, :, None], axis=1), "tp")
    spread = (selector[:, :, None] * low[:, None, :]).reshape(slots, holder * rank)
    stacked = up_stored.reshape(holder * rank, -1).astype(F32)
    term = jnp.dot(spread, stacked, precision=lax.Precision.HIGHEST).reshape(owners, cap, -1)
    term = lax.all_to_all(term, "own", split_axis=0, concat_axis=0, tiled=True).reshape(slots, -1)[dest]
    mixed = lax.psum_scatter(base, "tp", scatter_dimension=1, tiled=True) + ADAPTER_SCALE * term
    return mixed.astype(BF16)


def per_device(tokens, token_adapter_index, adapter_storage_row, value_matrix, down_stored, up_stored):
    owners, parts = lax.axis_size("own"), lax.axis_size("tp")
    count, features = tokens.shape
    cap = CAP * (2 * count // CAP // owners)
    on_a_line = owners == LINE and parts > 1 and parts & (parts - 1) == 0
    whole_tiles = cap % 256 == 0 and up_stored.shape[2] == 128 and features >= 3 * lanes(cap + 16) + 128
    countable = adapter_storage_row.shape[0] < 256 and cap + 16 <= CODE_ROWS * 128
    body = direct if on_a_line and whole_tiles and countable else by_all_to_all
    return body(tokens, token_adapter_index, adapter_storage_row, value_matrix, down_stored, up_stored)


def solution(mesh):
    return jax.shard_map(
        per_device,
        mesh=mesh,
        in_specs=(
            P(("rep", "own"), "tp"),
            P(("rep", "own")),
            P("rep"),
            P("tp", None),
            P(("rep", "own"), "tp", None),
            P(("rep", "own"), None, "tp"),
        ),
        out_specs=P(("rep", "own"), "tp"),
        check_vma=False,
    )
```

```python
import functools

import jax
import jax.numpy as jnp
from jax import lax
from jax.experimental import pallas as pl
from jax.experimental.pallas import tpu as pltpu
from jax.sharding import PartitionSpec as P

CAP = 4
ADAPTER_SCALE = 0.5
CODE_ROWS = 16
LINE = 4
BF16 = jnp.bfloat16
F32 = jnp.float32
VMEM_LIMIT = 16 * 2**20
CHEAP = pl.CostEstimate(flops=1, bytes_accessed=1, transcendentals=0)


def params(**kw):
    return pltpu.CompilerParams(vmem_limit_bytes=VMEM_LIMIT, **kw)


def iota(shape, dim):
    return lax.broadcasted_iota(jnp.int32, shape, dim)


def dot(a, b, dims=((1,), (0,))):
    return lax.dot_general(a, b, (dims, ((), ())), preferred_element_type=F32)


def split_bf16(x):
    high = x.astype(BF16)
    return high, (x - high.astype(F32)).astype(BF16)


def one_hot(mask):
    return mask.astype(F32).astype(BF16)


IN_VMEM = pl.BlockSpec(memory_space=pltpu.VMEM)
IN_SMEM = pl.BlockSpec(memory_space=pltpu.SMEM)


def storage_of(index_row, storage_row):
    adapters = storage_row.shape[1]
    square = (adapters, adapters)
    diagonal = jnp.where(iota(square, 0) == iota(square, 1), storage_row.astype(F32), 0.0)
    column = jnp.sum(diagonal, axis=1, keepdims=True)
    shape = (adapters, index_row.shape[1])
    picked = jnp.where(iota(shape, 0) == index_row, column, 0.0)
    return jnp.sum(picked, axis=0, keepdims=True).astype(jnp.int32)


def owner_of(storage, holder, owners):
    owner = jnp.zeros_like(storage)
    for k in range(1, owners):
        owner = owner + (storage >= k * holder).astype(jnp.int32)
    return owner


def earlier(tokens):
    return one_hot(iota((tokens, tokens), 0) < iota((tokens, tokens), 1))


def routes(index_row, storage_row, holder, owners, group, first, strict):
    tokens = index_row.shape[1]
    storage = storage_of(index_row, storage_row)
    owner = owner_of(storage, holder, owners)
    rows = -(-owners // 8) * 8
    hits = iota((rows, tokens), 0) == owner
    rank = jnp.sum(jnp.where(hits, dot(one_hot(hits), strict), 0.0), axis=0, keepdims=True)
    late = jnp.where((owner != group) & (rank >= first), 1.0, 0.0)
    place = dot(jnp.broadcast_to(late, (8, tokens)).astype(BF16), strict)[0:1, :]
    late_place = jnp.where(late > 0, place, -1.0).astype(jnp.int32)
    return owner, storage, rank.astype(jnp.int32), late_place


def lanes(count):
    return -(-count // 128) * 128


def known_adapters(storage, picks, flag, features):
    tokens = storage.shape[1]
    known = jnp.broadcast_to((storage + 1).astype(F32), (8, tokens)).astype(BF16)
    sections = []
    for pick in picks:
        size = pick.shape[0]
        sections.append(dot(known, pick, ((1,), (1,))))
        if size % 128:
            sections.append(jnp.zeros((8, lanes(size) - size), F32))
    used = sum(x.shape[1] for x in sections)
    sections += [jnp.full((8, 128), flag, F32), jnp.zeros((8, features - used - 128), F32)]
    return jnp.concatenate(sections, axis=1)[0:1, :]


def last_row(rows, row):
    return rows + jnp.where(iota(rows.shape, 0) == rows.shape[0] - 1, row, 0.0)


def route_pack_kernel(owners, holder, first, late, me_ref, index_hbm, storage_hbm, tokens_hbm, *refs):
    out, dest_ref, home_ids_ref, more_ref, picks, tags, index, storage, tokens, sems = refs
    tiles, _, tile = tokens.shape
    small = [pltpu.make_async_copy(index_hbm, index, sems.at[tiles])]
    small += [pltpu.make_async_copy(storage_hbm, storage, sems.at[tiles + 1])]
    large = [
        pltpu.make_async_copy(tokens_hbm.at[:, pl.ds(i * tile, tile)], tokens.at[i], sems.at[i])
        for i in range(tiles)
    ]
    for copy in small + large:
        copy.start()
    strict = earlier(index.shape[1])
    for copy in small:
        copy.wait()
    me = me_ref[0]
    owner, row, rank, place = routes(index[...], storage[...], holder, owners, me, first, strict)
    home_ids_ref[...] = jnp.where(owner == me, row - me * holder, -1)
    away = owner - me
    away = jnp.where(away < 0, away + owners, away)
    dest = jnp.where(place >= 0, (owners - 1) * first + place, (away - 1) * first + rank)
    dest_ref[...] = jnp.where(away == 0, -1, dest)
    more = (jnp.max(place) >= late).astype(jnp.int32)
    more_ref[0] = more
    for s in range(1, owners):
        slot = jnp.where(place >= 0, jnp.where(place < late, first + place, -1), jnp.where(away == s, rank, -1))
        picks[s - 1] = one_hot(iota(picks.shape[1:], 0) == slot)
    features = out.shape[1]
    tags[...] = known_adapters(row, [picks[s - 1] for s in range(1, owners)], more.astype(F32), features)
    for i, copy in enumerate(large):
        copy.wait()
        at = slice(i * tile, (i + 1) * tile)
        out[:, at] = last_row(dot(picks[owners - 2], tokens[i]), tags[:, at]).astype(BF16)


def route_pack(me, index_row, storage_row, tokens, owners, holder, first, late):
    count, features = tokens.shape
    tiles = 2 if features % 512 == 0 else 1
    in_hbm = pl.BlockSpec(memory_space=pltpu.HBM)
    long = first + late + 1
    return pl.pallas_call(
        functools.partial(route_pack_kernel, owners, holder, first, late),
        out_shape=[jax.ShapeDtypeStruct((long, features), BF16)]
        + [jax.ShapeDtypeStruct((1, count), jnp.int32)] * 2
        + [jax.ShapeDtypeStruct((1,), jnp.int32)],
        in_specs=[IN_SMEM, in_hbm, in_hbm, in_hbm],
        out_specs=[IN_VMEM] * 3 + [IN_SMEM],
        scratch_shapes=[
            pltpu.VMEM((owners - 1, long, count), BF16),
            pltpu.VMEM((1, features), F32),
            pltpu.VMEM(index_row.shape, jnp.int32),
            pltpu.VMEM(storage_row.shape, jnp.int32),
            pltpu.VMEM((tiles, count, features // tiles), BF16),
            pltpu.SemaphoreType.DMA((tiles + 2,)),
        ],
        compiler_params=params(),
        cost_estimate=CHEAP,
        name="route_pack",
    )(me, index_row, storage_row, tokens)


def pack_more_kernel(first, dest_ref, tokens_ref, third_ref, one_out, two_out):
    dest = dest_ref[...]
    for s, out in ((1, one_out), (2, two_out)):
        pick = one_hot(iota((first, dest.shape[1]), 0) + (s - 1) * first == dest)
        out[0:first, :] = dot(pick, tokens_ref[...]).astype(BF16)
    one_out[first:, :] = third_ref[first:, :]


def pack_more(dest, tokens, third, first):
    return pl.pallas_call(
        functools.partial(pack_more_kernel, first),
        out_shape=[jax.ShapeDtypeStruct(third.shape, BF16), jax.ShapeDtypeStruct((first, tokens.shape[1]), BF16)],
        in_specs=[IN_VMEM] * 3,
        out_specs=[IN_VMEM] * 2,
        compiler_params=params(),
        cost_estimate=CHEAP,
        name="pack_more",
    )(dest, tokens, third)


def repack_kernel(start, index_ref, storage_ref, dest_ref, tokens_ref, out):
    rows = out.shape[0] - 1
    row = iota((rows + 1, dest_ref.shape[1]), 0)
    pick = one_hot((row < rows) & (row + start == dest_ref[...]))
    tags = known_adapters(storage_of(index_ref[...], storage_ref[...]), [pick], 0.0, out.shape[1])
    out[...] = last_row(dot(pick, tokens_ref[...]), tags).astype(BF16)


def repack(index_row, storage_row, dest, tokens, start, rows):
    return pl.pallas_call(
        functools.partial(repack_kernel, start),
        out_shape=jax.ShapeDtypeStruct((rows + 1, tokens.shape[1]), BF16),
        in_specs=[IN_VMEM] * 4,
        out_specs=IN_VMEM,
        compiler_params=params(),
        name="repack",
    )(index_row, storage_row, dest, tokens)


def low_rank_kernel(blocks, joined, holder, rank, me_ref, down_ref, *refs):
    out, ids_out, flag = refs[-3:]
    lead = me_ref[0] * holder + 1
    flags = jnp.zeros((1, 1), F32)
    for k, (rows, sources, tagged, section, flag_at, column) in enumerate(blocks):
        rows_in = functools.reduce(jnp.add, [refs[j][at : at + rows, :] for j, at in sources])
        every = dot(down_ref[...], rows_in, ((1,), (1,)))
        tags = [refs[j][refs[j].shape[0] - 16 :, 0 : flag_at + 128].astype(F32)[15:16, :] for j in tagged]
        tags = functools.reduce(jnp.add, tags)
        flags = jnp.maximum(flags, tags[:, flag_at : flag_at + 1])
        ids = tags[:, section + column : section + column + rows].astype(jnp.int32) - lead
        total = jnp.zeros((rank, rows), F32)
        for a in range(holder):
            total = total + jnp.where(ids == a, every[a * rank : (a + 1) * rank, :], 0.0)
        at = slice(column, column + rows)
        if joined:
            out[:, at] = total
            ids_out[:, at] = ids
        else:
            out[k * rank : (k + 1) * rank, :] = total
            ids_out[k : k + 1, :] = ids
    flag[0] = jnp.max(flags).astype(jnp.int32)


def low_rank(me, down, blocks, messages, holder, joined=False):
    rank = down.shape[0] // holder
    rows = sum(block[0] for block in blocks) if joined else blocks[0][0]
    number = 1 if joined else len(blocks)
    return pl.pallas_call(
        functools.partial(low_rank_kernel, blocks, joined, holder, rank),
        out_shape=[
            jax.ShapeDtypeStruct((number * rank, rows), F32),
            jax.ShapeDtypeStruct((number, rows), jnp.int32),
            jax.ShapeDtypeStruct((1,), jnp.int32),
        ],
        in_specs=[IN_SMEM] + [IN_VMEM] * (1 + len(messages)),
        out_specs=[IN_VMEM, IN_VMEM, IN_SMEM],
        compiler_params=params(),
        cost_estimate=CHEAP,
        name="low_rank",
    )(me, down, *messages)


def low_rank_home_kernel(holder, rank, ids_ref, down_ref, tokens_ref, out):
    every = dot(down_ref[...], tokens_ref[...], ((1,), (1,)))
    ids = ids_ref[...]
    total = jnp.zeros(out.shape, F32)
    for a in range(holder):
        total = total + jnp.where(ids == a, every[a * rank : (a + 1) * rank, :], 0.0)
    out[...] = total


def low_rank_home(ids, down, tokens, holder):
    rank = down.shape[0] // holder
    return pl.pallas_call(
        functools.partial(low_rank_home_kernel, holder, rank),
        out_shape=jax.ShapeDtypeStruct((rank, tokens.shape[0]), F32),
        in_specs=[IN_VMEM] * 3,
        out_specs=IN_VMEM,
        compiler_params=params(),
        cost_estimate=CHEAP,
        name="low_rank_home",
    )(ids, down, tokens)


def up_kernel(rows, holder, rank, ids_ref, up_ref, a_ref, b_ref, *outs):
    up = up_ref[...]
    for k, out in enumerate(outs):
        own = slice(k * rank, (k + 1) * rank)
        low = a_ref[own, :] + b_ref[own, :]
        ids = ids_ref[k : k + 1, :]
        spread = jnp.concatenate([jnp.where(ids == a, low, 0.0) for a in range(holder)], axis=0)
        high, rest = split_bf16(spread)
        out[...] = dot(high, up, ((0,), (0,))) + dot(rest, up, ((0,), (0,)))


def up_project(ids, up, a, b, holder):
    blocks, rows = ids.shape
    rank = up.shape[0] // holder
    return pl.pallas_call(
        functools.partial(up_kernel, rows, holder, rank),
        out_shape=[jax.ShapeDtypeStruct((rows, up.shape[1]), F32)] * blocks,
        in_specs=[IN_VMEM] * 4,
        out_specs=[IN_VMEM] * blocks,
        compiler_params=params(),
        cost_estimate=CHEAP,
        name="up_project",
    )(ids, up, a, b)


def up_coded_kernel(holder, rank, ids_ref, up_ref, a_ref, b_ref, *outs):
    up = up_ref[...]
    for k, out in enumerate(outs):
        own = slice(k * rank, (k + 1) * rank)
        low = a_ref[own, :] + b_ref[own, :]
        ids = ids_ref[k : k + 1, :]
        spread = jnp.concatenate([jnp.where(ids == a, low, 0.0) for a in range(holder)], axis=0)
        high, rest = split_bf16(spread)
        term = ADAPTER_SCALE * (dot(high, up, ((0,), (0,))) + dot(rest, up, ((0,), (0,))))
        largest = jnp.maximum(jnp.max(jnp.abs(term), axis=1, keepdims=True), 1e-30)
        exponent = jnp.floor(jnp.log2(largest)) + 1.0
        code = jnp.clip(jnp.round(term * jnp.exp2(15.0 - exponent)), -32767.0, 32767.0)
        rows = term.shape[0]
        out[0:rows, :] = code.astype(jnp.int32).astype(jnp.int16)
        square = (rows, lanes(rows))
        exponent = jnp.sum(jnp.where(iota(square, 0) == iota(square, 1), exponent, 0.0), axis=0, keepdims=True)
        tail = jnp.zeros((CODE_ROWS, 128), F32)
        for j in range(lanes(rows) // 128):
            tail = jnp.where(iota(tail.shape, 0) == j, exponent[:, j * 128 : (j + 1) * 128], tail)
        out[rows:, :] = tail.astype(jnp.int32).astype(jnp.int16)


def up_coded(ids, up, a, b, holder):
    blocks, rows = ids.shape
    rank = up.shape[0] // holder
    return pl.pallas_call(
        functools.partial(up_coded_kernel, holder, rank),
        out_shape=[jax.ShapeDtypeStruct((rows + CODE_ROWS, up.shape[1]), jnp.int16)] * blocks,
        in_specs=[IN_VMEM] * 4,
        out_specs=[IN_VMEM] * blocks,
        compiler_params=params(),
        cost_estimate=CHEAP,
        name="up_coded",
    )(ids, up, a, b)


def base_kernel(parts, me_ref, tokens_ref, value_ref, kept_ref, away_ref, full):
    width = full.shape[1] // parts
    full[...] = dot(tokens_ref[...], value_ref[...])
    for q in range(parts):
        block = me_ref[0] ^ q
        at = pl.ds(q // 2 * width, width)
        (away_ref if q % 2 else kept_ref)[:, at] = full[:, pl.ds(pl.multiple_of(block * width, width), width)]


def base_blocks(me, tokens, value, parts):
    count, columns = tokens.shape[0], value.shape[1]
    return pl.pallas_call(
        functools.partial(base_kernel, parts),
        out_shape=[jax.ShapeDtypeStruct((count, columns // 2), F32)] * 2,
        in_specs=[IN_SMEM, IN_VMEM, IN_VMEM],
        out_specs=[IN_VMEM, IN_VMEM],
        scratch_shapes=[pltpu.VMEM((count, columns), F32)],
        compiler_params=params(),
        cost_estimate=CHEAP,
        name="base_blocks",
    )(me, tokens, value)


def gather_add_kernel(ranges, terms, dest_ref, *refs):
    total = refs[0][...]
    for k in range(1, terms):
        total = total + refs[k][...]
    dest = dest_ref[...]
    for (start, rows, late_start), ref in zip(ranges, refs[terms:]):
        size = ref.shape[0] - CODE_ROWS
        tail = ref[size:, :].astype(jnp.int32).astype(F32)
        diagonal = iota((128, 128), 0) == iota((128, 128), 1)
        exponents = [
            jnp.sum(jnp.where(diagonal, tail[j : j + 1, :], 0.0), axis=1, keepdims=True)[0 : min(128, size - j * 128), :]
            for j in range(lanes(size) // 128)
        ]
        scale = jnp.exp2(jnp.concatenate(exponents, axis=0) - 15.0)
        values = ref[0:size, :].astype(jnp.int32).astype(F32) * scale
        row = iota((size, dest.shape[1]), 0)
        pick = one_hot(jnp.where(row < rows, row + start, row + (late_start - rows)) == dest)
        high, rest = split_bf16(values)
        total = total + (dot(pick, high, ((0,), (0,))) + dot(pick, rest, ((0,), (0,))))
    refs[-1][...] = total.astype(refs[-1].dtype)


def gather_add(dest, ranges, terms, returned, dtype):
    return pl.pallas_call(
        functools.partial(gather_add_kernel, ranges, len(terms)),
        out_shape=jax.ShapeDtypeStruct(terms[0].shape, dtype),
        in_specs=[IN_VMEM] * (1 + len(terms) + len(returned)),
        out_specs=IN_VMEM,
        compiler_params=params(),
        cost_estimate=CHEAP,
        name="gather_add",
    )(dest, *terms, *returned)


def along(x, pairs):
    return lax.ppermute(x, "own", pairs)


def shifted(x, shift):
    size = lax.axis_size("own")
    return along(x, [(i, (i + shift) % size) for i in range(size)])


def opposite(before, after):
    even = lax.axis_index("own") % 2 == 0
    return along(jnp.where(even, before, after), [(0, 1), (1, 0), (2, 3), (3, 2)])


def partner(x, bit):
    return lax.ppermute(x, "tp", [(i, i ^ bit) for i in range(lax.axis_size("tp"))])


def two_terms(x):
    bit = 1
    while 2 * bit < lax.axis_size("tp"):
        x = x + partner(x, bit)
        bit *= 2
    return x, partner(x, bit)


def base_terms(kept, away, parts):
    bit = 1
    while 2 * bit < parts:
        total = kept + partner(away, bit)
        blocks = jnp.split(total, parts // (2 * bit), axis=1)
        bit *= 2
        kept, away = (jnp.concatenate(blocks[k::2], axis=1) if len(blocks) > 2 else blocks[k] for k in range(2))
    return kept, partner(away, bit)


def direct(tokens, token_adapter_index, adapter_storage_row, value_matrix, down_stored, up_stored):
    owners, parts = lax.axis_size("own"), lax.axis_size("tp")
    count = tokens.shape[0]
    holder, _, rank = down_stored.shape
    cap = CAP * (2 * count // CAP // owners)
    first = cap * 9 // 16 // 16 * 16
    late = cap - first + 15
    me = lax.axis_index("own").astype(jnp.int32).reshape(1)
    me_part = lax.axis_index("tp").astype(jnp.int32).reshape(1)
    index_row = token_adapter_index.reshape(1, count)
    storage_row = adapter_storage_row.reshape(1, -1)
    down = jnp.swapaxes(down_stored, 1, 2).reshape(holder * rank, -1)
    up = up_stored.reshape(holder * rank, -1)
    shifts = list(range(1, owners))
    late_start = (owners - 1) * first

    mains = {s: ((s - 1) * first, first) for s in shifts}
    size = first + late + 1
    part = lanes(size)
    flag_at = 3 * part
    third, dest, home_ids, more = route_pack(me, index_row, storage_row, tokens, owners, holder, first, late)
    third, me_part, home_ids = lax.optimization_barrier((third, me_part, home_ids))
    above = shifted(third, 3)
    blocks = base_blocks(me_part, tokens, value_matrix, parts)
    blocks, dest = lax.optimization_barrier((blocks, dest))
    one, two = pack_more(dest, tokens, third, first)
    below = shifted(one, 1)
    base = base_terms(*blocks, parts)
    lows = two_terms(low_rank_home(home_ids, down, tokens, holder))
    (stays,) = up_project(home_ids, up, *lows, holder)
    total = gather_add(dest, [], [*base, ADAPTER_SCALE * stays], [], F32)
    rest, above, total = lax.optimization_barrier((two, above, total))
    across = shifted(rest, 2)

    def near_round(s, message):
        lows, ids, more = low_rank(me, down, [(size, [(0, 0)], [0], (s - 1) * part, flag_at, 0)], [message], holder)
        (done,) = up_coded(ids, up, *two_terms(lows), holder)
        return done, more

    above_done, above_more = near_round(3, above)
    above_back = shifted(above_done, -3)
    below, above_done = lax.optimization_barrier((below, above_done))
    far = opposite(below[first:], above[first:])
    below_done, below_more = near_round(1, below)
    near = [below_done, above_done]
    near_more = jnp.maximum(below_more, above_more)
    back = [shifted(below_done, -1), above_back]
    total = gather_add(dest, [(*mains[s], late_start) for s in (1, 3)], [total], back, F32)

    def second(total):
        x = repack(index_row, storage_row, dest, tokens, late_start + late, late)
        below, above = shifted(x, 1), shifted(x, 3)
        x = [below, opposite(below, above), above]
        sources = [[0], [1], [2]]
        blocks = [(late + 1, [(j, 0) for j in js], js, 0, lanes(late + 1), 0) for js in sources]
        lows, ids, _ = low_rank(me, down, blocks, x, holder)
        done = up_coded(ids, up, *two_terms(lows), holder)
        back = [shifted(x, -s) for s, x in zip(shifts, done)]
        return gather_add(dest, [(late_start + late, late + 1, 0)] * len(back), [total], back, F32)

    across, far, near = lax.optimization_barrier((across, far, near))
    joined = [
        (first, [(0, 0)], [1], part, flag_at, 0),
        (late + 1, [(1, 0)], [1], part, flag_at, first),
    ]
    lows, ids, far_more = low_rank(me, down, joined, [across, far], holder, joined=True)
    (done,) = up_coded(ids, up, *two_terms(lows), holder)
    more = jnp.maximum(more[0], jnp.maximum(near_more[0], far_more[0]))
    total = lax.cond(more > 0, second, lambda total: total, total)
    back = shifted(done, -2)
    return gather_add(dest, [(*mains[2], late_start)], [total], [back], BF16)


def by_all_to_all(tokens, token_adapter_index, adapter_storage_row, value_matrix, down_stored, up_stored):
    owners = lax.axis_size("own")
    tok_dev, features = tokens.shape
    holder, _, rank = down_stored.shape
    cap = CAP * (2 * tok_dev // CAP // owners)
    slots = owners * cap
    catalog = jnp.arange(adapter_storage_row.shape[0], dtype=jnp.int32)
    storage = jnp.sum(
        jnp.where(token_adapter_index[:, None] == catalog[None, :], adapter_storage_row[None, :], 0), axis=1
    )
    home_owner = storage // holder
    hits = (home_owner[:, None] == jnp.arange(owners, dtype=jnp.int32)[None, :]).astype(jnp.int32)
    before = jnp.cumsum(hits, axis=0) - hits
    dest = home_owner * cap + jnp.sum(before * hits, axis=1)
    outgoing = jnp.zeros((slots, features), tokens.dtype).at[dest].set(tokens)
    which = jnp.full((slots,), holder, jnp.int32).at[dest].set(storage % holder)
    base = jnp.dot(tokens, value_matrix, preferred_element_type=F32)
    rows_in = lax.all_to_all(
        outgoing.reshape(owners, cap, features), "own", split_axis=0, concat_axis=0, tiled=True
    ).reshape(slots, features)
    which = lax.all_to_all(which.reshape(owners, cap), "own", split_axis=0, concat_axis=0, tiled=True)
    selector = (which.reshape(slots)[:, None] == jnp.arange(holder)[None, :]).astype(F32)
    every = jnp.einsum("nf,afr->nar", rows_in, down_stored, preferred_element_type=F32)
    low = lax.psum(jnp.sum(every * selector[:, :, None], axis=1), "tp")
    spread = (selector[:, :, None] * low[:, None, :]).reshape(slots, holder * rank)
    stacked = up_stored.reshape(holder * rank, -1).astype(F32)
    term = jnp.dot(spread, stacked, precision=lax.Precision.HIGHEST).reshape(owners, cap, -1)
    term = lax.all_to_all(term, "own", split_axis=0, concat_axis=0, tiled=True).reshape(slots, -1)[dest]
    mixed = lax.psum_scatter(base, "tp", scatter_dimension=1, tiled=True) + ADAPTER_SCALE * term
    return mixed.astype(BF16)


def per_device(tokens, token_adapter_index, adapter_storage_row, value_matrix, down_stored, up_stored):
    owners, parts = lax.axis_size("own"), lax.axis_size("tp")
    count, features = tokens.shape
    cap = CAP * (2 * count // CAP // owners)
    on_a_line = owners == LINE and parts > 1 and parts & (parts - 1) == 0
    whole_tiles = cap % 256 == 0 and up_stored.shape[2] == 128 and features >= 3 * lanes(cap + 16) + 128
    countable = adapter_storage_row.shape[0] < 256 and cap + 16 <= CODE_ROWS * 128
    body = direct if on_a_line and whole_tiles and countable else by_all_to_all
    return body(tokens, token_adapter_index, adapter_storage_row, value_matrix, down_stored, up_stored)


def solution(mesh):
    return jax.shard_map(
        per_device,
        mesh=mesh,
        in_specs=(
            P(("rep", "own"), "tp"),
            P(("rep", "own")),
            P("rep"),
            P("tp", None),
            P(("rep", "own"), "tp", None),
            P(("rep", "own"), None, "tp"),
        ),
        out_specs=P(("rep", "own"), "tp"),
        check_vma=False,
    )
```

```python
import functools

import jax
import jax.numpy as jnp
from jax import lax
from jax.experimental import pallas as pl
from jax.experimental.pallas import tpu as pltpu
from jax.sharding import PartitionSpec as P

CAP = 4
ADAPTER_SCALE = 0.5
CODE_ROWS = 16
LINE = 4
BF16 = jnp.bfloat16
F32 = jnp.float32
VMEM_LIMIT = 16 * 2**20
CHEAP = pl.CostEstimate(flops=1, bytes_accessed=1, transcendentals=0)


def params(**kw):
    return pltpu.CompilerParams(vmem_limit_bytes=VMEM_LIMIT, **kw)


def iota(shape, dim):
    return lax.broadcasted_iota(jnp.int32, shape, dim)


def dot(a, b, dims=((1,), (0,))):
    return lax.dot_general(a, b, (dims, ((), ())), preferred_element_type=F32)


def split_bf16(x):
    high = x.astype(BF16)
    return high, (x - high.astype(F32)).astype(BF16)


def one_hot(mask):
    return mask.astype(F32).astype(BF16)


IN_VMEM = pl.BlockSpec(memory_space=pltpu.VMEM)
IN_SMEM = pl.BlockSpec(memory_space=pltpu.SMEM)


def storage_of(index_row, storage_row):
    adapters = storage_row.shape[1]
    square = (adapters, adapters)
    diagonal = jnp.where(iota(square, 0) == iota(square, 1), storage_row.astype(F32), 0.0)
    column = jnp.sum(diagonal, axis=1, keepdims=True)
    shape = (adapters, index_row.shape[1])
    picked = jnp.where(iota(shape, 0) == index_row, column, 0.0)
    return jnp.sum(picked, axis=0, keepdims=True).astype(jnp.int32)


def owner_of(storage, holder, owners):
    owner = jnp.zeros_like(storage)
    for k in range(1, owners):
        owner = owner + (storage >= k * holder).astype(jnp.int32)
    return owner


def earlier(tokens):
    return one_hot(iota((tokens, tokens), 0) < iota((tokens, tokens), 1))


def routes(index_row, storage_row, holder, owners, group, first, strict):
    tokens = index_row.shape[1]
    storage = storage_of(index_row, storage_row)
    owner = owner_of(storage, holder, owners)
    rows = -(-owners // 8) * 8
    hits = iota((rows, tokens), 0) == owner
    rank = jnp.sum(jnp.where(hits, dot(one_hot(hits), strict), 0.0), axis=0, keepdims=True)
    late = jnp.where((owner != group) & (rank >= first), 1.0, 0.0)
    place = dot(jnp.broadcast_to(late, (8, tokens)).astype(BF16), strict)[0:1, :]
    late_place = jnp.where(late > 0, place, -1.0).astype(jnp.int32)
    return owner, storage, rank.astype(jnp.int32), late_place


def lanes(count):
    return -(-count // 128) * 128


def known_adapters(storage, picks, flag, features):
    tokens = storage.shape[1]
    known = jnp.broadcast_to((storage + 1).astype(F32), (8, tokens)).astype(BF16)
    sections = []
    for pick in picks:
        size = pick.shape[0]
        sections.append(dot(known, pick, ((1,), (1,))))
        if size % 128:
            sections.append(jnp.zeros((8, lanes(size) - size), F32))
    used = sum(x.shape[1] for x in sections)
    sections += [jnp.full((8, 128), flag, F32), jnp.zeros((8, features - used - 128), F32)]
    return jnp.concatenate(sections, axis=1)[0:1, :]


def last_row(rows, row):
    return rows + jnp.where(iota(rows.shape, 0) == rows.shape[0] - 1, row, 0.0)


def route_pack_kernel(owners, holder, first, late, me_ref, index_hbm, storage_hbm, tokens_hbm, *refs):
    out, dest_ref, home_ids_ref, more_ref, picks, tags, index, storage, tokens, sems = refs
    tiles, _, tile = tokens.shape
    small = [pltpu.make_async_copy(index_hbm, index, sems.at[tiles])]
    small += [pltpu.make_async_copy(storage_hbm, storage, sems.at[tiles + 1])]
    large = [
        pltpu.make_async_copy(tokens_hbm.at[:, pl.ds(i * tile, tile)], tokens.at[i], sems.at[i])
        for i in range(tiles)
    ]
    for copy in small + large:
        copy.start()
    strict = earlier(index.shape[1])
    for copy in small:
        copy.wait()
    me = me_ref[0]
    owner, row, rank, place = routes(index[...], storage[...], holder, owners, me, first, strict)
    home_ids_ref[...] = jnp.where(owner == me, row - me * holder, -1)
    away = owner - me
    away = jnp.where(away < 0, away + owners, away)
    dest = jnp.where(place >= 0, (owners - 1) * first + place, (away - 1) * first + rank)
    dest_ref[...] = jnp.where(away == 0, -1, dest)
    more = (jnp.max(place) >= late).astype(jnp.int32)
    more_ref[0] = more
    for s in range(1, owners):
        slot = jnp.where(place >= 0, jnp.where(place < late, first + place, -1), jnp.where(away == s, rank, -1))
        picks[s - 1] = one_hot(iota(picks.shape[1:], 0) == slot)
    features = out.shape[1]
    tags[...] = known_adapters(row, [picks[s - 1] for s in range(1, owners)], more.astype(F32), features)
    for i, copy in enumerate(large):
        copy.wait()
        at = slice(i * tile, (i + 1) * tile)
        out[:, at] = last_row(dot(picks[owners - 2], tokens[i]), tags[:, at]).astype(BF16)


def route_pack(me, index_row, storage_row, tokens, owners, holder, first, late):
    count, features = tokens.shape
    tiles = 1
    in_hbm = pl.BlockSpec(memory_space=pltpu.HBM)
    long = first + late + 1
    return pl.pallas_call(
        functools.partial(route_pack_kernel, owners, holder, first, late),
        out_shape=[jax.ShapeDtypeStruct((long, features), BF16)]
        + [jax.ShapeDtypeStruct((1, count), jnp.int32)] * 2
        + [jax.ShapeDtypeStruct((1,), jnp.int32)],
        in_specs=[IN_SMEM, in_hbm, in_hbm, in_hbm],
        out_specs=[IN_VMEM] * 3 + [IN_SMEM],
        scratch_shapes=[
            pltpu.VMEM((owners - 1, long, count), BF16),
            pltpu.VMEM((1, features), F32),
            pltpu.VMEM(index_row.shape, jnp.int32),
            pltpu.VMEM(storage_row.shape, jnp.int32),
            pltpu.VMEM((tiles, count, features // tiles), BF16),
            pltpu.SemaphoreType.DMA((tiles + 2,)),
        ],
        compiler_params=params(),
        cost_estimate=CHEAP,
        name="route_pack",
    )(me, index_row, storage_row, tokens)


def pack_more_kernel(first, dest_ref, tokens_ref, third_ref, one_out, two_out):
    dest = dest_ref[...]
    for s, out in ((1, one_out), (2, two_out)):
        pick = one_hot(iota((first, dest.shape[1]), 0) + (s - 1) * first == dest)
        out[0:first, :] = dot(pick, tokens_ref[...]).astype(BF16)
    one_out[first:, :] = third_ref[first:, :]


def pack_more(dest, tokens, third, first):
    return pl.pallas_call(
        functools.partial(pack_more_kernel, first),
        out_shape=[jax.ShapeDtypeStruct(third.shape, BF16), jax.ShapeDtypeStruct((first, tokens.shape[1]), BF16)],
        in_specs=[IN_VMEM] * 3,
        out_specs=[IN_VMEM] * 2,
        compiler_params=params(),
        cost_estimate=CHEAP,
        name="pack_more",
    )(dest, tokens, third)


def repack_kernel(start, index_ref, storage_ref, dest_ref, tokens_ref, out):
    rows = out.shape[0] - 1
    row = iota((rows + 1, dest_ref.shape[1]), 0)
    pick = one_hot((row < rows) & (row + start == dest_ref[...]))
    tags = known_adapters(storage_of(index_ref[...], storage_ref[...]), [pick], 0.0, out.shape[1])
    out[...] = last_row(dot(pick, tokens_ref[...]), tags).astype(BF16)


def repack(index_row, storage_row, dest, tokens, start, rows):
    return pl.pallas_call(
        functools.partial(repack_kernel, start),
        out_shape=jax.ShapeDtypeStruct((rows + 1, tokens.shape[1]), BF16),
        in_specs=[IN_VMEM] * 4,
        out_specs=IN_VMEM,
        compiler_params=params(),
        name="repack",
    )(index_row, storage_row, dest, tokens)


def low_rank_kernel(blocks, joined, holder, rank, me_ref, down_ref, *refs):
    out, ids_out, flag = refs[-3:]
    lead = me_ref[0] * holder + 1
    flags = jnp.zeros((1, 1), F32)
    for k, (rows, sources, tagged, section, flag_at, column) in enumerate(blocks):
        rows_in = functools.reduce(jnp.add, [refs[j][at : at + rows, :] for j, at in sources])
        every = dot(down_ref[...], rows_in, ((1,), (1,)))
        tags = [refs[j][refs[j].shape[0] - 16 :, 0 : flag_at + 128].astype(F32)[15:16, :] for j in tagged]
        tags = functools.reduce(jnp.add, tags)
        flags = jnp.maximum(flags, tags[:, flag_at : flag_at + 1])
        ids = tags[:, section + column : section + column + rows].astype(jnp.int32) - lead
        total = jnp.zeros((rank, rows), F32)
        for a in range(holder):
            total = total + jnp.where(ids == a, every[a * rank : (a + 1) * rank, :], 0.0)
        at = slice(column, column + rows)
        if joined:
            out[:, at] = total
            ids_out[:, at] = ids
        else:
            out[k * rank : (k + 1) * rank, :] = total
            ids_out[k : k + 1, :] = ids
    flag[0] = jnp.max(flags).astype(jnp.int32)


def low_rank(me, down, blocks, messages, holder, joined=False):
    rank = down.shape[0] // holder
    rows = sum(block[0] for block in blocks) if joined else blocks[0][0]
    number = 1 if joined else len(blocks)
    return pl.pallas_call(
        functools.partial(low_rank_kernel, blocks, joined, holder, rank),
        out_shape=[
            jax.ShapeDtypeStruct((number * rank, rows), F32),
            jax.ShapeDtypeStruct((number, rows), jnp.int32),
            jax.ShapeDtypeStruct((1,), jnp.int32),
        ],
        in_specs=[IN_SMEM] + [IN_VMEM] * (1 + len(messages)),
        out_specs=[IN_VMEM, IN_VMEM, IN_SMEM],
        compiler_params=params(),
        cost_estimate=CHEAP,
        name="low_rank",
    )(me, down, *messages)


def low_rank_home_kernel(holder, rank, ids_ref, down_ref, tokens_ref, out):
    every = dot(down_ref[...], tokens_ref[...], ((1,), (1,)))
    ids = ids_ref[...]
    total = jnp.zeros(out.shape, F32)
    for a in range(holder):
        total = total + jnp.where(ids == a, every[a * rank : (a + 1) * rank, :], 0.0)
    out[...] = total


def low_rank_home(ids, down, tokens, holder):
    rank = down.shape[0] // holder
    return pl.pallas_call(
        functools.partial(low_rank_home_kernel, holder, rank),
        out_shape=jax.ShapeDtypeStruct((rank, tokens.shape[0]), F32),
        in_specs=[IN_VMEM] * 3,
        out_specs=IN_VMEM,
        compiler_params=params(),
        cost_estimate=CHEAP,
        name="low_rank_home",
    )(ids, down, tokens)


def up_kernel(rows, holder, rank, ids_ref, up_ref, a_ref, b_ref, *outs):
    up = up_ref[...]
    for k, out in enumerate(outs):
        own = slice(k * rank, (k + 1) * rank)
        low = a_ref[own, :] + b_ref[own, :]
        ids = ids_ref[k : k + 1, :]
        spread = jnp.concatenate([jnp.where(ids == a, low, 0.0) for a in range(holder)], axis=0)
        high, rest = split_bf16(spread)
        out[...] = dot(high, up, ((0,), (0,))) + dot(rest, up, ((0,), (0,)))


def up_project(ids, up, a, b, holder):
    blocks, rows = ids.shape
    rank = up.shape[0] // holder
    return pl.pallas_call(
        functools.partial(up_kernel, rows, holder, rank),
        out_shape=[jax.ShapeDtypeStruct((rows, up.shape[1]), F32)] * blocks,
        in_specs=[IN_VMEM] * 4,
        out_specs=[IN_VMEM] * blocks,
        compiler_params=params(),
        cost_estimate=CHEAP,
        name="up_project",
    )(ids, up, a, b)


def up_coded_kernel(holder, rank, ids_ref, up_ref, a_ref, b_ref, *outs):
    up = up_ref[...]
    for k, out in enumerate(outs):
        own = slice(k * rank, (k + 1) * rank)
        low = a_ref[own, :] + b_ref[own, :]
        ids = ids_ref[k : k + 1, :]
        spread = jnp.concatenate([jnp.where(ids == a, low, 0.0) for a in range(holder)], axis=0)
        high, rest = split_bf16(spread)
        term = ADAPTER_SCALE * (dot(high, up, ((0,), (0,))) + dot(rest, up, ((0,), (0,))))
        largest = jnp.maximum(jnp.max(jnp.abs(term), axis=1, keepdims=True), 1e-30)
        exponent = jnp.floor(jnp.log2(largest)) + 1.0
        code = jnp.clip(jnp.round(term * jnp.exp2(15.0 - exponent)), -32767.0, 32767.0)
        rows = term.shape[0]
        out[0:rows, :] = code.astype(jnp.int32).astype(jnp.int16)
        square = (rows, lanes(rows))
        exponent = jnp.sum(jnp.where(iota(square, 0) == iota(square, 1), exponent, 0.0), axis=0, keepdims=True)
        tail = jnp.zeros((CODE_ROWS, 128), F32)
        for j in range(lanes(rows) // 128):
            tail = jnp.where(iota(tail.shape, 0) == j, exponent[:, j * 128 : (j + 1) * 128], tail)
        out[rows:, :] = tail.astype(jnp.int32).astype(jnp.int16)


def up_coded(ids, up, a, b, holder):
    blocks, rows = ids.shape
    rank = up.shape[0] // holder
    return pl.pallas_call(
        functools.partial(up_coded_kernel, holder, rank),
        out_shape=[jax.ShapeDtypeStruct((rows + CODE_ROWS, up.shape[1]), jnp.int16)] * blocks,
        in_specs=[IN_VMEM] * 4,
        out_specs=[IN_VMEM] * blocks,
        compiler_params=params(),
        cost_estimate=CHEAP,
        name="up_coded",
    )(ids, up, a, b)


def base_kernel(parts, me_ref, tokens_ref, value_ref, kept_ref, away_ref, full):
    width = full.shape[1] // parts
    full[...] = dot(tokens_ref[...], value_ref[...])
    for q in range(parts):
        block = me_ref[0] ^ q
        at = pl.ds(q // 2 * width, width)
        (away_ref if q % 2 else kept_ref)[:, at] = full[:, pl.ds(pl.multiple_of(block * width, width), width)]


def base_blocks(me, tokens, value, parts):
    count, columns = tokens.shape[0], value.shape[1]
    return pl.pallas_call(
        functools.partial(base_kernel, parts),
        out_shape=[jax.ShapeDtypeStruct((count, columns // 2), F32)] * 2,
        in_specs=[IN_SMEM, IN_VMEM, IN_VMEM],
        out_specs=[IN_VMEM, IN_VMEM],
        scratch_shapes=[pltpu.VMEM((count, columns), F32)],
        compiler_params=params(),
        cost_estimate=CHEAP,
        name="base_blocks",
    )(me, tokens, value)


def gather_add_kernel(ranges, terms, dest_ref, *refs):
    total = refs[0][...]
    for k in range(1, terms):
        total = total + refs[k][...]
    dest = dest_ref[...]
    for (start, rows, late_start), ref in zip(ranges, refs[terms:]):
        size = ref.shape[0] - CODE_ROWS
        tail = ref[size:, :].astype(jnp.int32).astype(F32)
        diagonal = iota((128, 128), 0) == iota((128, 128), 1)
        exponents = [
            jnp.sum(jnp.where(diagonal, tail[j : j + 1, :], 0.0), axis=1, keepdims=True)[0 : min(128, size - j * 128), :]
            for j in range(lanes(size) // 128)
        ]
        scale = jnp.exp2(jnp.concatenate(exponents, axis=0) - 15.0)
        values = ref[0:size, :].astype(jnp.int32).astype(F32) * scale
        row = iota((size, dest.shape[1]), 0)
        pick = one_hot(jnp.where(row < rows, row + start, row + (late_start - rows)) == dest)
        high, rest = split_bf16(values)
        total = total + (dot(pick, high, ((0,), (0,))) + dot(pick, rest, ((0,), (0,))))
    refs[-1][...] = total.astype(refs[-1].dtype)


def gather_add(dest, ranges, terms, returned, dtype):
    return pl.pallas_call(
        functools.partial(gather_add_kernel, ranges, len(terms)),
        out_shape=jax.ShapeDtypeStruct(terms[0].shape, dtype),
        in_specs=[IN_VMEM] * (1 + len(terms) + len(returned)),
        out_specs=IN_VMEM,
        compiler_params=params(),
        cost_estimate=CHEAP,
        name="gather_add",
    )(dest, *terms, *returned)


def along(x, pairs):
    return lax.ppermute(x, "own", pairs)


def shifted(x, shift):
    size = lax.axis_size("own")
    return along(x, [(i, (i + shift) % size) for i in range(size)])


def opposite(before, after):
    even = lax.axis_index("own") % 2 == 0
    return along(jnp.where(even, before, after), [(0, 1), (1, 0), (2, 3), (3, 2)])


def partner(x, bit):
    return lax.ppermute(x, "tp", [(i, i ^ bit) for i in range(lax.axis_size("tp"))])


def two_terms(x):
    bit = 1
    while 2 * bit < lax.axis_size("tp"):
        x = x + partner(x, bit)
        bit *= 2
    return x, partner(x, bit)


def base_terms(kept, away, parts):
    bit = 1
    while 2 * bit < parts:
        total = kept + partner(away, bit)
        blocks = jnp.split(total, parts // (2 * bit), axis=1)
        bit *= 2
        kept, away = (jnp.concatenate(blocks[k::2], axis=1) if len(blocks) > 2 else blocks[k] for k in range(2))
    return kept, partner(away, bit)


def direct(tokens, token_adapter_index, adapter_storage_row, value_matrix, down_stored, up_stored):
    owners, parts = lax.axis_size("own"), lax.axis_size("tp")
    count = tokens.shape[0]
    holder, _, rank = down_stored.shape
    cap = CAP * (2 * count // CAP // owners)
    first = cap * 9 // 16 // 16 * 16
    late = cap - first + 15
    me = lax.axis_index("own").astype(jnp.int32).reshape(1)
    me_part = lax.axis_index("tp").astype(jnp.int32).reshape(1)
    index_row = token_adapter_index.reshape(1, count)
    storage_row = adapter_storage_row.reshape(1, -1)
    down = jnp.swapaxes(down_stored, 1, 2).reshape(holder * rank, -1)
    up = up_stored.reshape(holder * rank, -1)
    shifts = list(range(1, owners))
    late_start = (owners - 1) * first

    mains = {s: ((s - 1) * first, first) for s in shifts}
    size = first + late + 1
    part = lanes(size)
    flag_at = 3 * part
    third, dest, home_ids, more = route_pack(me, index_row, storage_row, tokens, owners, holder, first, late)
    third, me_part, home_ids = lax.optimization_barrier((third, me_part, home_ids))
    above = shifted(third, 3)
    blocks = base_blocks(me_part, tokens, value_matrix, parts)
    blocks, dest = lax.optimization_barrier((blocks, dest))
    one, two = pack_more(dest, tokens, third, first)
    below = shifted(one, 1)
    base = base_terms(*blocks, parts)
    lows = two_terms(low_rank_home(home_ids, down, tokens, holder))
    (stays,) = up_project(home_ids, up, *lows, holder)
    total = gather_add(dest, [], [*base, ADAPTER_SCALE * stays], [], F32)
    rest, above, total = lax.optimization_barrier((two, above, total))
    across = shifted(rest, 2)

    def near_round(s, message):
        lows, ids, more = low_rank(me, down, [(size, [(0, 0)], [0], (s - 1) * part, flag_at, 0)], [message], holder)
        (done,) = up_coded(ids, up, *two_terms(lows), holder)
        return done, more

    above_done, above_more = near_round(3, above)
    above_back = shifted(above_done, -3)
    below, above_done = lax.optimization_barrier((below, above_done))
    far = opposite(below[first:], above[first:])
    below_done, below_more = near_round(1, below)
    near = [below_done, above_done]
    near_more = jnp.maximum(below_more, above_more)
    back = [shifted(below_done, -1), above_back]
    total = gather_add(dest, [(*mains[s], late_start) for s in (1, 3)], [total], back, F32)

    def second(total):
        x = repack(index_row, storage_row, dest, tokens, late_start + late, late)
        below, above = shifted(x, 1), shifted(x, 3)
        x = [below, opposite(below, above), above]
        sources = [[0], [1], [2]]
        blocks = [(late + 1, [(j, 0) for j in js], js, 0, lanes(late + 1), 0) for js in sources]
        lows, ids, _ = low_rank(me, down, blocks, x, holder)
        done = up_coded(ids, up, *two_terms(lows), holder)
        back = [shifted(x, -s) for s, x in zip(shifts, done)]
        return gather_add(dest, [(late_start + late, late + 1, 0)] * len(back), [total], back, F32)

    across, far, below_done = lax.optimization_barrier((across, far, below_done))
    joined = [
        (first, [(0, 0)], [1], part, flag_at, 0),
        (late + 1, [(1, 0)], [1], part, flag_at, first),
    ]
    lows, ids, far_more = low_rank(me, down, joined, [across, far], holder, joined=True)
    (done,) = up_coded(ids, up, *two_terms(lows), holder)
    more = jnp.maximum(more[0], jnp.maximum(near_more[0], far_more[0]))
    total = lax.cond(more > 0, second, lambda total: total, total)
    back = shifted(done, -2)
    return gather_add(dest, [(*mains[2], late_start)], [total], [back], BF16)


def by_all_to_all(tokens, token_adapter_index, adapter_storage_row, value_matrix, down_stored, up_stored):
    owners = lax.axis_size("own")
    tok_dev, features = tokens.shape
    holder, _, rank = down_stored.shape
    cap = CAP * (2 * tok_dev // CAP // owners)
    slots = owners * cap
    catalog = jnp.arange(adapter_storage_row.shape[0], dtype=jnp.int32)
    storage = jnp.sum(
        jnp.where(token_adapter_index[:, None] == catalog[None, :], adapter_storage_row[None, :], 0), axis=1
    )
    home_owner = storage // holder
    hits = (home_owner[:, None] == jnp.arange(owners, dtype=jnp.int32)[None, :]).astype(jnp.int32)
    before = jnp.cumsum(hits, axis=0) - hits
    dest = home_owner * cap + jnp.sum(before * hits, axis=1)
    outgoing = jnp.zeros((slots, features), tokens.dtype).at[dest].set(tokens)
    which = jnp.full((slots,), holder, jnp.int32).at[dest].set(storage % holder)
    base = jnp.dot(tokens, value_matrix, preferred_element_type=F32)
    rows_in = lax.all_to_all(
        outgoing.reshape(owners, cap, features), "own", split_axis=0, concat_axis=0, tiled=True
    ).reshape(slots, features)
    which = lax.all_to_all(which.reshape(owners, cap), "own", split_axis=0, concat_axis=0, tiled=True)
    selector = (which.reshape(slots)[:, None] == jnp.arange(holder)[None, :]).astype(F32)
    every = jnp.einsum("nf,afr->nar", rows_in, down_stored, preferred_element_type=F32)
    low = lax.psum(jnp.sum(every * selector[:, :, None], axis=1), "tp")
    spread = (selector[:, :, None] * low[:, None, :]).reshape(slots, holder * rank)
    stacked = up_stored.reshape(holder * rank, -1).astype(F32)
    term = jnp.dot(spread, stacked, precision=lax.Precision.HIGHEST).reshape(owners, cap, -1)
    term = lax.all_to_all(term, "own", split_axis=0, concat_axis=0, tiled=True).reshape(slots, -1)[dest]
    mixed = lax.psum_scatter(base, "tp", scatter_dimension=1, tiled=True) + ADAPTER_SCALE * term
    return mixed.astype(BF16)


def per_device(tokens, token_adapter_index, adapter_storage_row, value_matrix, down_stored, up_stored):
    owners, parts = lax.axis_size("own"), lax.axis_size("tp")
    count, features = tokens.shape
    cap = CAP * (2 * count // CAP // owners)
    on_a_line = owners == LINE and parts > 1 and parts & (parts - 1) == 0
    whole_tiles = cap % 256 == 0 and up_stored.shape[2] == 128 and features >= 3 * lanes(cap + 16) + 128
    countable = adapter_storage_row.shape[0] < 256 and cap + 16 <= CODE_ROWS * 128
    body = direct if on_a_line and whole_tiles and countable else by_all_to_all
    return body(tokens, token_adapter_index, adapter_storage_row, value_matrix, down_stored, up_stored)


def solution(mesh):
    return jax.shard_map(
        per_device,
        mesh=mesh,
        in_specs=(
            P(("rep", "own"), "tp"),
            P(("rep", "own")),
            P("rep"),
            P("tp", None),
            P(("rep", "own"), "tp", None),
            P(("rep", "own"), None, "tp"),
        ),
        out_specs=P(("rep", "own"), "tp"),
        check_vma=False,
    )
```
